32 devices in a mesh: corner: 8 (over y, x, core), tm: 4 (over z).
Axes of the slice: x: 2, y: 2, z: 4, core: 2. Of those that a mesh axis runs over, the one named last changes fastest.
Arguments:
- signal: bfloat16 [8, 64, 16384], P('corner', None, 'tm'), may hold values from -6 to 6
- dilated_conv_weight: bfloat16 [2, 256, 128], replicated, may hold values from -0.5 to 0.5
- dilated_conv_bias: float32 [2, 256], replicated, may hold values from -3 to 3
- projection_weight: bfloat16 [2, 128, 128], replicated, may hold values from -0.5 to 0.5
- projection_bias: float32 [2, 128], replicated, may hold values from -3 to 3
- cot_top: bfloat16 [8, 64, 16384], P('corner', None, 'tm'), may hold values from -6 to 6
- cot_skip: bfloat16 [8, 64, 16384], P('corner', None, 'tm'), may hold values from -6 to 6
Outputs:
- x_top: bfloat16 [8, 64, 16384], P('corner', None, 'tm')
- skip_sum: bfloat16 [8, 64, 16384], P('corner', None, 'tm')
- grad_input: bfloat16 [8, 64, 16384], P('corner', None, 'tm')
- grad_conv: float32 [2, 256, 128], replicated
- grad_conv_bias: float32 [2, 256], replicated
- grad_out: float32 [2, 128, 128], replicated
- grad_out_bias: float32 [2, 128], replicated
The draws below stay inside these ranges and needn't reach their ends.
All inputs are finite; a program needn't handle non-finite values.
Results may differ from the reference program's by a relative error of at most 0.0065.
Values may be sent and summed in bfloat16 or wider, within the bound.
A program may use at most 64 MiB of HBM per device.

```python
import math
import jax
import jax.numpy as jnp
from jax import lax

R = 64
G = 128
SKIP = 64
LAYERS = 2
CORNERS = 8
TIME = 16384
LOWER_DILATION = 4096
UPPER_DILATION = 8192


def levels(key, dims, cuts, smallest, largest):
    level, own = 1.0, jax.random.fold_in(key, 6)
    for position, parts in cuts:
        steps = jnp.exp(jax.random.uniform(jax.random.fold_in(own, position), (parts,), jnp.float32, smallest / len(cuts), largest / len(cuts)))
        level = level * jnp.repeat(steps, dims[position] // parts).reshape([-1 if axis == position else 1 for axis in range(len(dims))])
    return level


def scatter_about(rng, extent, spread, limit, cuts=(), kind=jnp.bfloat16):
    factor_of = levels(rng, extent, cuts, -0.22, 0.18) if cuts else 1.0
    array = jax.random.normal(rng, extent, jnp.float32) * spread * factor_of
    return jnp.minimum(jnp.maximum(array, -limit), limit).astype(kind)


def setup_inputs(seed: int = 0) -> dict:
    key_list = jax.random.split(jax.random.key(seed), 8)
    signal = scatter_about(key_list[0], (CORNERS, R, TIME), 1.0, 6.0, ((0, 8), (2, 4)))
    dilated_conv_weight = scatter_about(key_list[1], (LAYERS, 2 * G, 2 * R), (2 * R) ** -0.5, 0.5)
    dilated_conv_bias = scatter_about(key_list[2], (LAYERS, 2 * G), 0.5, 3.0, (), jnp.float32)
    projection_weight = scatter_about(key_list[3], (LAYERS, R + SKIP, G), G ** -0.5, 0.5)
    projection_bias = scatter_about(key_list[4], (LAYERS, R + SKIP), 0.5, 3.0, (), jnp.float32)
    cot_top = scatter_about(key_list[5], (CORNERS, R, TIME), 1.0, 6.0, ((0, 8), (2, 4)))
    cot_skip = scatter_about(key_list[6], (CORNERS, SKIP, TIME), 1.0, 6.0, ((0, 8), (2, 4)))
    return dict(signal=signal, dilated_conv_weight=dilated_conv_weight, dilated_conv_bias=dilated_conv_bias, projection_weight=projection_weight, projection_bias=projection_bias, cot_top=cot_top, cot_skip=cot_skip)


def shift_delayed(field, shift):
    zeros = jnp.zeros((field.shape[0], shift), field.dtype)
    return jnp.concatenate([zeros, field[:, :field.shape[1] - shift]], axis=1)

def shift_forward(field, shift):
    zeros = jnp.zeros((field.shape[0], shift), field.dtype)
    return jnp.concatenate([field[:, shift:], zeros], axis=1)

def gated_layer_forward(a_in, tap_in, weight, bias, proj, proj_bias):
    stacked = jnp.concatenate([tap_in, a_in], axis=0)
    pre_act = jnp.dot(weight, stacked, preferred_element_type=jnp.float32) + bias[:, None]
    gate_out = (jnp.tanh(pre_act[:G]) * jax.nn.sigmoid(pre_act[G:])).astype(jnp.bfloat16)
    mixed = jnp.dot(proj, gate_out, preferred_element_type=jnp.float32) + proj_bias[:, None]
    next_act = (a_in.astype(jnp.float32) + mixed[:R]).astype(jnp.bfloat16)
    return (stacked, pre_act, gate_out, next_act, mixed[R:])

def layer_backward(go_res, go_skip, stacked, pre_act, gate_out, weight, proj):
    upper = jnp.concatenate([go_res, go_skip], axis=0)
    grad_proj = jnp.dot(upper, gate_out.T, preferred_element_type=jnp.float32)
    grad_pbias = lax.optimization_barrier(jnp.sum(upper.astype(jnp.float32), axis=1))
    grad_gate = jnp.dot(proj.T, upper, preferred_element_type=jnp.float32)
    filt_act = jnp.tanh(pre_act[:G])
    gate_act = jax.nn.sigmoid(pre_act[G:])
    grad_pre = jnp.concatenate([grad_gate * gate_act * (1.0 - filt_act * filt_act), grad_gate * filt_act * gate_act * (1.0 - gate_act)], axis=0).astype(jnp.bfloat16)
    grad_weight = jnp.dot(grad_pre, stacked.T, preferred_element_type=jnp.float32)
    grad_bias = lax.optimization_barrier(jnp.sum(grad_pre.astype(jnp.float32), axis=1))
    grad_in = jnp.dot(weight.T, grad_pre, preferred_element_type=jnp.float32)
    return (grad_in[:R].astype(jnp.bfloat16), grad_in[R:], grad_weight, grad_bias, grad_proj, grad_pbias)

def reference(signal, dilated_conv_weight, dilated_conv_bias, projection_weight, projection_bias, cot_top, cot_skip):

    def one_corner(items):
        lower_layer_input, upper_output_gradient, skip_cot = items
        lower_saved_state, lower_preactivation, lower_gated_output, middle_layer_input, lower_skip_output = gated_layer_forward(lower_layer_input, shift_delayed(lower_layer_input, LOWER_DILATION), dilated_conv_weight[0], dilated_conv_bias[0], projection_weight[0], projection_bias[0])
        upper_saved_state, upper_preactivation, upper_gated_output, upper_layer_output, upper_skip_output = gated_layer_forward(middle_layer_input, shift_delayed(middle_layer_input, UPPER_DILATION), dilated_conv_weight[1], dilated_conv_bias[1], projection_weight[1], projection_bias[1])
        skip_out = (lower_skip_output + upper_skip_output).astype(jnp.bfloat16)
        delayed_gradient_upper, current_gradient_upper, gw_top, gb_top, gv_top, gcb_top = layer_backward(upper_output_gradient, skip_cot, upper_saved_state, upper_preactivation, upper_gated_output, dilated_conv_weight[1], projection_weight[1])
        middle_input_gradient = (upper_output_gradient.astype(jnp.float32) + current_gradient_upper + shift_forward(delayed_gradient_upper, UPPER_DILATION).astype(jnp.float32)).astype(jnp.bfloat16)
        delayed_gradient_lower, current_gradient_lower, gw_low, gb_low, gv_low, gcb_low = layer_backward(middle_input_gradient, skip_cot, lower_saved_state, lower_preactivation, lower_gated_output, dilated_conv_weight[0], projection_weight[0])
        lower_input_gradient = (middle_input_gradient.astype(jnp.float32) + current_gradient_lower + shift_forward(delayed_gradient_lower, LOWER_DILATION).astype(jnp.float32)).astype(jnp.bfloat16)
        return (upper_layer_output, skip_out, lower_input_gradient, jnp.stack([gw_low, gw_top]), jnp.stack([gb_low, gb_top]), jnp.stack([gv_low, gv_top]), jnp.stack([gcb_low, gcb_top]))
    outs = lax.map(one_corner, (signal, cot_top, cot_skip))
    scale = 1.0 / math.sqrt(CORNERS * TIME)
    return (outs[0], outs[1], outs[2], lax.optimization_barrier(jnp.sum(outs[3], axis=0)) * scale, lax.optimization_barrier(jnp.sum(outs[4], axis=0)) * scale, lax.optimization_barrier(jnp.sum(outs[5], axis=0)) * scale, lax.optimization_barrier(jnp.sum(outs[6], axis=0)) * scale)
```

```python
import functools
import math

import jax
import jax.numpy as jnp
from jax import lax
from jax.experimental import pallas as pl
from jax.experimental.pallas import tpu as pltpu
from jax.sharding import PartitionSpec as P

MESH = pl.DeviceIdType.MESH
F32 = jnp.float32
BF16 = jnp.bfloat16
CHUNK = 512


def dot(a, b):
    return jnp.dot(a, b, preferred_element_type=F32)


def dot_nt(a, b):
    return lax.dot_general(a, b, (((1,), (1,)), ((), ())), preferred_element_type=F32)


def kernel(
    cfg,
    sig,
    w,
    wb,
    p,
    pb,
    ct,
    cs,
    xtop,
    skip,
    ginp,
    gconv,
    gcbias,
    gout,
    gobias,
    tap0,
    xmid,
    tap1,
    gdel1,
    d1,
    gdel0,
    d0,
    df0,
    dg0,
    z0,
    skip0,
    res1,
    res0,
    wt,
    pt,
    wbc,
    pbc,
    accw,
    accp,
    part,
    rs_buf,
    z_buf,
    total,
    sig_s,
    sig_r,
    x_s,
    x_r,
    d1_s,
    d1_r,
    d0_s,
    d0_r,
    rs_s,
    rs_r,
    z_s,
    z_r,
    ag_s,
    ag_r,
):
    ncor, ntm, nc, t, rows, scale = cfg
    r = sig.shape[1]
    g = p.shape[2]
    g2 = w.shape[1]
    po = p.shape[1]
    me = lax.axis_index("corner")
    zi = lax.axis_index("tm")

    def cols(i):
        return pl.ds(pl.multiple_of(i * t, t), t)

    def shift_copy(src, dst, ssem, rsem, i, distance):
        return pltpu.make_async_remote_copy(
            src_ref=src,
            dst_ref=dst.at[i],
            send_sem=ssem.at[i],
            recv_sem=rsem.at[i],
            device_id={"tm": lax.rem(zi + distance + ntm, ntm)},
            device_id_type=MESH,
        )

    def sig_copy(i):
        return shift_copy(sig.at[0, :, cols(i)], tap0, sig_s, sig_r, i, 1)

    def x_copy(i):
        return shift_copy(xmid.at[i], tap1, x_s, x_r, i, 2)

    def d1_copy(i):
        return shift_copy(gdel1.at[i], d1, d1_s, d1_r, i, -2)

    def d0_copy(i):
        return shift_copy(gdel0.at[i], d0, d0_s, d0_r, i, -1)

    barrier = pltpu.get_barrier_semaphore()

    def greet_corner(j, carry):
        pl.semaphore_signal(
            barrier, inc=1, device_id={"corner": lax.rem(me + j, ncor)}, device_id_type=MESH
        )
        return carry

    def greet_tm(j, carry):
        pl.semaphore_signal(
            barrier, inc=1, device_id={"tm": lax.rem(zi + j, ntm)}, device_id_type=MESH
        )
        return carry

    lax.fori_loop(1, ncor, greet_corner, 0)
    lax.fori_loop(1, ntm, greet_tm, 0)

    for l in range(2):
        wt[l] = w[l].astype(F32).T.astype(BF16)
        pt[l] = p[l].astype(F32).T.astype(BF16)
        wbc[l] = jnp.broadcast_to(wb[l : l + 1, :], (128, g2)).T
        pbc[l] = jnp.broadcast_to(pb[l : l + 1, :], (128, po)).T
    accw[...] = jnp.zeros_like(accw)
    accp[...] = jnp.zeros_like(accp)
    part[...] = jnp.zeros_like(part)

    @pl.when(zi < 1)
    def _():
        tap0[...] = jnp.zeros_like(tap0)

    @pl.when(zi < 2)
    def _():
        tap1[...] = jnp.zeros_like(tap1)

    @pl.when(zi >= ntm - 2)
    def _():
        d1[...] = jnp.zeros_like(d1)

    @pl.when(zi >= ntm - 1)
    def _():
        d0[...] = jnp.zeros_like(d0)

    pl.semaphore_wait(barrier, ncor - 1 + ntm - 1)

    @pl.when(zi < ntm - 1)
    def _():
        def send(i, carry):
            sig_copy(i).start()
            return carry

        lax.fori_loop(0, nc, send, 0)

    ones = jnp.ones((128, t), BF16)

    def wide(ref, l):
        return jnp.concatenate([ref[l]] * (t // 128), axis=1)

    def gates(l, stacked):
        pre = dot(w[l], stacked) + wide(wbc, l)
        th = jnp.tanh(pre[:g])
        sg = 0.5 * jnp.tanh(0.5 * pre[g:]) + 0.5
        z = th * sg
        zb = z.astype(BF16)
        mixed = dot(p[l], zb) + wide(pbc, l)
        return sg - z * th, z - z * sg, zb, mixed

    def accumulate(l, gpre, stacked, u, zb):
        accw[l] += dot_nt(gpre, jnp.concatenate([stacked, ones], axis=0))
        accp[l] += dot_nt(u, jnp.concatenate([zb, ones], axis=0))

    def forward_low(i, carry):
        @pl.when(zi >= 1)
        def _():
            sig_copy(i).wait_recv()

        a = sig[0, :, cols(i)]
        df, dg, zb, mixed = gates(0, jnp.concatenate([tap0[i], a], axis=0))
        xmid[i] = (a.astype(F32) + mixed[:r]).astype(BF16)

        @pl.when(zi < ntm - 2)
        def _():
            x_copy(i).start()

        df0[i] = df
        dg0[i] = dg
        z0[i] = zb
        skip0[i] = mixed[r:]
        return carry

    def top(i, carry):
        @pl.when(zi >= 2)
        def _():
            x_copy(i).wait_recv()

        a = xmid[i]
        stacked = jnp.concatenate([tap1[i], a], axis=0)
        df, dg, zb, mixed = gates(1, stacked)
        c = ct[0, :, cols(i)]
        u = jnp.concatenate([c, cs[0, :, cols(i)]], axis=0)
        gz = dot(pt[1], u)
        gpre = jnp.concatenate([gz * df, gz * dg], axis=0).astype(BF16)
        gin = dot(wt[1], gpre)
        gdel1[i] = gin[:r].astype(BF16)

        @pl.when(zi >= 2)
        def _():
            d1_copy(i).start()

        res1[i] = c.astype(F32) + gin[r:]
        xtop[0, :, cols(i)] = (a.astype(F32) + mixed[:r]).astype(BF16)
        skip[0, :, cols(i)] = (skip0[i] + mixed[r:]).astype(BF16)
        accumulate(1, gpre, stacked, u, zb)
        return carry

    def backward_low(i, carry):
        @pl.when(zi < ntm - 2)
        def _():
            d1_copy(i).wait_recv()

        gm = (res1[i] + d1[i].astype(F32)).astype(BF16)
        u = jnp.concatenate([gm, cs[0, :, cols(i)]], axis=0)
        gz = dot(pt[0], u)
        gpre = jnp.concatenate([gz * df0[i], gz * dg0[i]], axis=0).astype(BF16)
        gin = dot(wt[0], gpre)
        gdel0[i] = gin[:r].astype(BF16)

        @pl.when(zi >= 1)
        def _():
            d0_copy(i).start()

        res0[i] = gm.astype(F32) + gin[r:]
        stacked = jnp.concatenate([tap0[i], sig[0, :, cols(i)]], axis=0)
        accumulate(0, gpre, stacked, u, z0[i])
        return carry

    def finish(i, carry):
        @pl.when(zi < ntm - 1)
        def _():
            d0_copy(i).wait_recv()

        ginp[0, :, cols(i)] = (res0[i] + d0[i].astype(F32)).astype(BF16)
        return carry

    def shard(k):
        return pl.ds(pl.multiple_of(k * rows, 8), rows)

    def rs_copy(l, j):
        to = lax.rem(me + j, ncor)
        return pltpu.make_async_remote_copy(
            src_ref=part.at[l, shard(to)],
            dst_ref=rs_buf.at[l, j - 1],
            send_sem=rs_s.at[l, j - 1],
            recv_sem=rs_r.at[l, j - 1],
            device_id={"corner": to},
            device_id_type=MESH,
        )

    def z_copy(l, j):
        return pltpu.make_async_remote_copy(
            src_ref=z_buf.at[l, zi],
            dst_ref=z_buf.at[l, zi],
            send_sem=z_s.at[l, j - 1],
            recv_sem=z_r.at[l, j - 1],
            device_id={"tm": lax.rem(zi + j, ntm)},
            device_id_type=MESH,
        )

    def z_arrival(l, j):
        origin = lax.rem(zi - j + ntm, ntm)
        return pltpu.make_async_remote_copy(
            src_ref=z_buf.at[l, zi],
            dst_ref=z_buf.at[l, origin],
            send_sem=z_s.at[l, j - 1],
            recv_sem=z_r.at[l, j - 1],
            device_id={"tm": lax.rem(zi + j, ntm)},
            device_id_type=MESH,
        )

    def ag_copy(l, j):
        return pltpu.make_async_remote_copy(
            src_ref=total.at[l, shard(me)],
            dst_ref=total.at[l, shard(me)],
            send_sem=ag_s.at[l, j - 1],
            recv_sem=ag_r.at[l, j - 1],
            device_id={"corner": lax.rem(me + j, ncor)},
            device_id_type=MESH,
        )

    def ag_arrival(l, j):
        return pltpu.make_async_remote_copy(
            src_ref=total.at[l, shard(me)],
            dst_ref=total.at[l, shard(lax.rem(me - j + ncor, ncor))],
            send_sem=ag_s.at[l, j - 1],
            recv_sem=ag_r.at[l, j - 1],
            device_id={"corner": lax.rem(me + j, ncor)},
            device_id_type=MESH,
        )

    def each(n, body):
        def step(j, carry):
            body(j)
            return carry

        lax.fori_loop(1, n, step, 0)

    def rs_start(l):
        part[l, 0:g2] = accw[l, :, 0:128]
        part[l, g2 : g2 + po] = accp[l, :, 0:128]
        brow = accw[l, :, 128:256].T
        for k in range(g2 // 128):
            part[l, g2 + po + k : g2 + po + k + 1] = brow[0:1, k * 128 : (k + 1) * 128]
        prow = accp[l, :, 128:256].T
        at = g2 + po + g2 // 128
        part[l, at : at + 1] = prow[0:1, :]
        each(ncor, lambda j: rs_copy(l, j).start())

    def z_start(l):
        each(ncor, lambda j: rs_copy(l, j).wait_recv())
        s = part[l, shard(me)]
        for j in range(ncor - 1):
            s = s + rs_buf[l, j]
        z_buf[l, zi] = s
        each(ntm, lambda j: z_copy(l, j).start())

    def ag_start(l):
        each(ntm, lambda j: z_arrival(l, j).wait_recv())
        s = z_buf[l, 0]
        for j in range(1, ntm):
            s = s + z_buf[l, j]
        total[l, shard(me)] = s * scale
        each(ncor, lambda j: ag_copy(l, j).start())

    def ag_finish(l):
        each(ncor, lambda j: ag_arrival(l, j).wait_recv())
        gconv[l] = total[l, 0:g2]
        gout[l] = total[l, g2 : g2 + po]
        for k in range(g2 // 128):
            gcbias[l : l + 1, k * 128 : (k + 1) * 128] = total[l, g2 + po + k : g2 + po + k + 1]
        at = g2 + po + g2 // 128
        gobias[l : l + 1, :] = total[l, at : at + 1]

    lax.fori_loop(0, nc, forward_low, 0)
    lax.fori_loop(0, nc, top, 0)
    rs_start(1)
    lax.fori_loop(0, nc // 2, backward_low, 0)
    z_start(1)
    lax.fori_loop(nc // 2, nc, backward_low, 0)
    rs_start(0)
    ag_start(1)
    z_start(0)
    lax.fori_loop(0, nc, finish, 0)
    ag_start(0)
    ag_finish(1)
    ag_finish(0)

    def sent(i, carry):
        @pl.when(zi < ntm - 1)
        def _():
            sig_copy(i).wait_send()

        @pl.when(zi < ntm - 2)
        def _():
            x_copy(i).wait_send()

        @pl.when(zi >= 2)
        def _():
            d1_copy(i).wait_send()

        @pl.when(zi >= 1)
        def _():
            d0_copy(i).wait_send()

        return carry

    lax.fori_loop(0, nc, sent, 0)
    for l in range(2):
        each(ncor, lambda j: rs_copy(l, j).wait_send())
        each(ntm, lambda j: z_copy(l, j).wait_send())
        each(ncor, lambda j: ag_copy(l, j).wait_send())


def on_device(sig, w, wb, p, pb, ct, cs):
    ncor = lax.axis_size("corner")
    ntm = lax.axis_size("tm")
    _, r, time = sig.shape
    _, g2, _ = w.shape
    _, po, g = p.shape
    t = CHUNK
    nc = time // t
    used = g2 + po + g2 // 128 + 1
    rows = -(-used // (ncor * 8)) * 8
    count = sig.shape[0] * ncor * time * ntm
    cfg = (ncor, ntm, nc, t, rows, 1.0 / math.sqrt(count))
    vmem = pl.BlockSpec(memory_space=pltpu.VMEM)
    dma = pltpu.SemaphoreType.DMA
    field = pltpu.VMEM((nc, r, t), BF16)
    field32 = pltpu.VMEM((nc, r, t), F32)
    flops = 2 * 2 * time * 3 * (g2 * 2 * r + po * g)
    return pl.pallas_call(
        functools.partial(kernel, cfg),
        out_shape=(
            jax.ShapeDtypeStruct(sig.shape, BF16),
            jax.ShapeDtypeStruct(sig.shape, BF16),
            jax.ShapeDtypeStruct(sig.shape, BF16),
            jax.ShapeDtypeStruct(w.shape, F32),
            jax.ShapeDtypeStruct(wb.shape, F32),
            jax.ShapeDtypeStruct(p.shape, F32),
            jax.ShapeDtypeStruct(pb.shape, F32),
        ),
        in_specs=[vmem] * 7,
        out_specs=[vmem] * 7,
        scratch_shapes=[
            field,
            field,
            field,
            field,
            field,
            field,
            field,
            pltpu.VMEM((nc, g, t), F32),
            pltpu.VMEM((nc, g, t), F32),
            pltpu.VMEM((nc, g, t), BF16),
            field32,
            field32,
            field32,
            pltpu.VMEM((2, w.shape[2], g2), BF16),
            pltpu.VMEM((2, g, po), BF16),
            pltpu.VMEM((2, g2, 128), F32),
            pltpu.VMEM((2, po, 128), F32),
            pltpu.VMEM((2, g2, 256), F32),
            pltpu.VMEM((2, po, 256), F32),
            pltpu.VMEM((2, ncor * rows, 128), F32),
            pltpu.VMEM((2, ncor - 1, rows, 128), F32),
            pltpu.VMEM((2, ntm, rows, 128), F32),
            pltpu.VMEM((2, ncor * rows, 128), F32),
        ]
        + [dma((nc,))] * 8
        + [dma((2, ncor - 1))] * 2
        + [dma((2, ntm - 1))] * 2
        + [dma((2, ncor - 1))] * 2,
        compiler_params=pltpu.CompilerParams(
            collective_id=0, has_side_effects=True, vmem_limit_bytes=48 * 1024 * 1024
        ),
        cost_estimate=pl.CostEstimate(
            flops=flops, bytes_accessed=6 * sig.size * 2, transcendentals=2 * g2 * time
        ),
    )(sig, w, wb, p, pb, ct, cs)


def solution(mesh):
    field = P("corner", None, "tm")
    return jax.shard_map(
        on_device,
        mesh=mesh,
        in_specs=(field, P(), P(), P(), P(), field, field),
        out_specs=(field, field, field, P(), P(), P(), P()),
        check_vma=False,
    )
```

```python
import functools
import math

import jax
import jax.numpy as jnp
from jax import lax
from jax.experimental import pallas as pl
from jax.experimental.pallas import tpu as pltpu
from jax.sharding import PartitionSpec as P

MESH = pl.DeviceIdType.MESH
F32 = jnp.float32
BF16 = jnp.bfloat16
CHUNK = 512
LAG = 2


def dot(a, b):
    return jnp.dot(a, b, preferred_element_type=F32)


def dot_nt(a, b):
    return lax.dot_general(a, b, (((1,), (1,)), ((), ())), preferred_element_type=F32)


def kernel(
    cfg,
    sig_h,
    w_h,
    wb_h,
    p_h,
    pb_h,
    ct_h,
    cs_h,
    xtop_h,
    skip_h,
    ginp_h,
    gconv_h,
    gcbias_h,
    gout_h,
    gobias_h,
    sig,
    w,
    wb,
    p,
    pb,
    ct,
    cs,
    in_s,
    xtop,
    skip,
    ginp,
    gcbias,
    gobias,
    out_s,
    tap0,
    xmid,
    tap1,
    gdel1,
    d1,
    gdel0,
    d0,
    df0,
    dg0,
    z0,
    skip0,
    res1,
    res0,
    wt,
    pt,
    wbc,
    pbc,
    accw,
    accp,
    part,
    rs_buf,
    z_buf,
    total,
    sig_s,
    sig_r,
    x_s,
    x_r,
    d1_s,
    d1_r,
    d0_s,
    d0_r,
    rs_s,
    rs_r,
    z_s,
    z_r,
    ag_s,
    ag_r,
):
    ncor, ntm, nc, t, rows, scale = cfg
    lag = min(LAG, nc)
    r = sig.shape[1]
    g = p.shape[2]
    g2 = w.shape[1]
    po = p.shape[1]
    me = lax.axis_index("corner")
    zi = lax.axis_index("tm")

    def cols(i):
        return pl.ds(pl.multiple_of(i * t, t), t)

    def shift_copy(src, dst, ssem, rsem, i, distance):
        return pltpu.make_async_remote_copy(
            src_ref=src,
            dst_ref=dst.at[i],
            send_sem=ssem.at[i],
            recv_sem=rsem.at[i],
            device_id={"tm": lax.rem(zi + distance + ntm, ntm)},
            device_id_type=MESH,
        )

    def sig_copy(i):
        return shift_copy(sig.at[0, :, cols(i)], tap0, sig_s, sig_r, i, 1)

    def x_copy(i):
        return shift_copy(xmid.at[i], tap1, x_s, x_r, i, 2)

    def d1_copy(i):
        return shift_copy(gdel1.at[i], d1, d1_s, d1_r, i, -2)

    def d0_copy(i):
        return shift_copy(gdel0.at[i], d0, d0_s, d0_r, i, -1)

    moves = [
        pltpu.make_async_copy(a, b, in_s.at[k])
        for k, (a, b) in enumerate(
            ((sig_h, sig), (w_h, w), (wb_h, wb), (p_h, p), (pb_h, pb), (ct_h, ct), (cs_h, cs))
        )
    ]
    for m in moves:
        m.start()

    barrier = pltpu.get_barrier_semaphore()

    def greet_corner(j, carry):
        pl.semaphore_signal(
            barrier, inc=1, device_id={"corner": lax.rem(me + j, ncor)}, device_id_type=MESH
        )
        return carry

    def greet_tm(j, carry):
        pl.semaphore_signal(
            barrier, inc=1, device_id={"tm": lax.rem(zi + j, ntm)}, device_id_type=MESH
        )
        return carry

    lax.fori_loop(1, ncor, greet_corner, 0)
    lax.fori_loop(1, ntm, greet_tm, 0)

    for m in moves:
        m.wait()
    for l in range(2):
        wt[l] = w[l].astype(F32).T.astype(BF16)
        pt[l] = p[l].astype(F32).T.astype(BF16)
        wbc[l] = jnp.broadcast_to(wb[l : l + 1, :], (128, g2)).T
        pbc[l] = jnp.broadcast_to(pb[l : l + 1, :], (128, po)).T
    accw[...] = jnp.zeros_like(accw)
    accp[...] = jnp.zeros_like(accp)
    part[...] = jnp.zeros_like(part)

    @pl.when(zi < 1)
    def _():
        tap0[...] = jnp.zeros_like(tap0)

    @pl.when(zi < 2)
    def _():
        tap1[...] = jnp.zeros_like(tap1)

    @pl.when(zi >= ntm - 2)
    def _():
        d1[...] = jnp.zeros_like(d1)

    @pl.when(zi >= ntm - 1)
    def _():
        d0[...] = jnp.zeros_like(d0)

    pl.semaphore_wait(barrier, ncor - 1 + ntm - 1)

    @pl.when(zi < ntm - 1)
    def _():
        def send(i, carry):
            sig_copy(i).start()
            return carry

        lax.fori_loop(0, nc, send, 0)

    ones = jnp.ones((128, t), BF16)

    def wide(ref, l):
        return jnp.concatenate([ref[l]] * (t // 128), axis=1)

    def gates(l, stacked):
        pre = dot(w[l], stacked) + wide(wbc, l)
        th = jnp.tanh(pre[:g])
        sg = 0.5 * jnp.tanh(0.5 * pre[g:]) + 0.5
        z = th * sg
        zb = z.astype(BF16)
        mixed = dot(p[l], zb) + wide(pbc, l)
        return sg - z * th, z - z * sg, zb, mixed

    def accumulate(l, gpre, stacked, u, zb):
        accw[l] += dot_nt(gpre, jnp.concatenate([stacked, ones], axis=0))
        accp[l] += dot_nt(u, jnp.concatenate([zb, ones], axis=0))

    def forward_low(i, carry):
        @pl.when(zi >= 1)
        def _():
            sig_copy(i).wait_recv()

        a = sig[0, :, cols(i)]
        df, dg, zb, mixed = gates(0, jnp.concatenate([tap0[i], a], axis=0))
        xmid[i] = (a.astype(F32) + mixed[:r]).astype(BF16)
        df0[i] = df
        dg0[i] = dg
        z0[i] = zb
        skip0[i] = mixed[r:]

        @pl.when(zi < ntm - 2)
        def _():
            x_copy(i).start()

        return carry

    def wait_x(i):
        @pl.when(zi >= 2)
        def _():
            x_copy(i).wait_recv()

    def send_d1(i):
        @pl.when(zi >= 2)
        def _():
            d1_copy(i).start()

    def wait_d1(i):
        @pl.when(zi < ntm - 2)
        def _():
            d1_copy(i).wait_recv()

    def send_d0(i):
        @pl.when(zi >= 1)
        def _():
            d0_copy(i).start()

    def top(i):
        a = xmid[i]
        stacked = jnp.concatenate([tap1[i], a], axis=0)
        df, dg, zb, mixed = gates(1, stacked)
        c = ct[0, :, cols(i)]
        u = jnp.concatenate([c, cs[0, :, cols(i)]], axis=0)
        gz = dot(pt[1], u)
        gpre = jnp.concatenate([gz * df, gz * dg], axis=0).astype(BF16)
        gin = dot(wt[1], gpre)
        gdel1[i] = gin[:r].astype(BF16)
        res1[i] = c.astype(F32) + gin[r:]
        xtop[0, :, cols(i)] = (a.astype(F32) + mixed[:r]).astype(BF16)
        skip[0, :, cols(i)] = (skip0[i] + mixed[r:]).astype(BF16)
        accumulate(1, gpre, stacked, u, zb)

    def low(i):
        gm = (res1[i] + d1[i].astype(F32)).astype(BF16)
        u = jnp.concatenate([gm, cs[0, :, cols(i)]], axis=0)
        gz = dot(pt[0], u)
        gpre = jnp.concatenate([gz * df0[i], gz * dg0[i]], axis=0).astype(BF16)
        gin = dot(wt[0], gpre)
        gdel0[i] = gin[:r].astype(BF16)
        res0[i] = gm.astype(F32) + gin[r:]
        stacked = jnp.concatenate([tap0[i], sig[0, :, cols(i)]], axis=0)
        accumulate(0, gpre, stacked, u, z0[i])

    def top_only(i, carry):
        wait_x(i)
        top(i)
        send_d1(i)
        return carry

    def both(i, carry):
        wait_x(i)
        wait_d1(i - lag)
        low(i - lag)
        top(i)
        send_d1(i)
        send_d0(i - lag)
        return carry

    def low_only(i, carry):
        wait_d1(i)
        low(i)
        send_d0(i)
        return carry

    def finish(i, carry):
        @pl.when(zi < ntm - 1)
        def _():
            d0_copy(i).wait_recv()

        ginp[0, :, cols(i)] = (res0[i] + d0[i].astype(F32)).astype(BF16)
        return carry

    def shard(k):
        return pl.ds(pl.multiple_of(k * rows, 8), rows)

    def rs_copy(l, j):
        to = lax.rem(me + j, ncor)
        return pltpu.make_async_remote_copy(
            src_ref=part.at[l, shard(to)],
            dst_ref=rs_buf.at[l, j - 1],
            send_sem=rs_s.at[l, j - 1],
            recv_sem=rs_r.at[l, j - 1],
            device_id={"corner": to},
            device_id_type=MESH,
        )

    def z_copy(l, j):
        return pltpu.make_async_remote_copy(
            src_ref=z_buf.at[l, zi],
            dst_ref=z_buf.at[l, zi],
            send_sem=z_s.at[l, j - 1],
            recv_sem=z_r.at[l, j - 1],
            device_id={"tm": lax.rem(zi + j, ntm)},
            device_id_type=MESH,
        )

    def z_arrival(l, j):
        origin = lax.rem(zi - j + ntm, ntm)
        return pltpu.make_async_remote_copy(
            src_ref=z_buf.at[l, zi],
            dst_ref=z_buf.at[l, origin],
            send_sem=z_s.at[l, j - 1],
            recv_sem=z_r.at[l, j - 1],
            device_id={"tm": lax.rem(zi + j, ntm)},
            device_id_type=MESH,
        )

    def ag_copy(l, j):
        return pltpu.make_async_remote_copy(
            src_ref=total.at[l, shard(me)],
            dst_ref=total.at[l, shard(me)],
            send_sem=ag_s.at[l, j - 1],
            recv_sem=ag_r.at[l, j - 1],
            device_id={"corner": lax.rem(me + j, ncor)},
            device_id_type=MESH,
        )

    def ag_arrival(l, j):
        return pltpu.make_async_remote_copy(
            src_ref=total.at[l, shard(me)],
            dst_ref=total.at[l, shard(lax.rem(me - j + ncor, ncor))],
            send_sem=ag_s.at[l, j - 1],
            recv_sem=ag_r.at[l, j - 1],
            device_id={"corner": lax.rem(me + j, ncor)},
            device_id_type=MESH,
        )

    def put(src, dst, k):
        return pltpu.make_async_copy(src, dst, out_s.at[k])

    def each(n, body):
        def step(j, carry):
            body(j)
            return carry

        lax.fori_loop(1, n, step, 0)

    def rs_start(l):
        part[l, 0:g2] = accw[l, :, 0:128]
        part[l, g2 : g2 + po] = accp[l, :, 0:128]
        brow = accw[l, :, 128:256].T
        for k in range(g2 // 128):
            part[l, g2 + po + k : g2 + po + k + 1] = brow[0:1, k * 128 : (k + 1) * 128]
        prow = accp[l, :, 128:256].T
        at = g2 + po + g2 // 128
        part[l, at : at + 1] = prow[0:1, :]
        each(ncor, lambda j: rs_copy(l, j).start())

    def z_start(l):
        each(ncor, lambda j: rs_copy(l, j).wait_recv())
        s = part[l, shard(me)]
        for j in range(ncor - 1):
            s = s + rs_buf[l, j]
        z_buf[l, zi] = s
        each(ntm, lambda j: z_copy(l, j).start())

    def ag_start(l):
        each(ntm, lambda j: z_arrival(l, j).wait_recv())
        s = z_buf[l, 0]
        for j in range(1, ntm):
            s = s + z_buf[l, j]
        total[l, shard(me)] = s * scale
        each(ncor, lambda j: ag_copy(l, j).start())

    def ag_finish(l):
        each(ncor, lambda j: ag_arrival(l, j).wait_recv())
        put(total.at[l, 0:g2], gconv_h.at[l], 5 + l).start()
        put(total.at[l, g2 : g2 + po], gout_h.at[l], 7 + l).start()
        for k in range(g2 // 128):
            gcbias[l : l + 1, k * 128 : (k + 1) * 128] = total[l, g2 + po + k : g2 + po + k + 1]
        at = g2 + po + g2 // 128
        gobias[l : l + 1, :] = total[l, at : at + 1]

    lax.fori_loop(0, nc, forward_low, 0)
    lax.fori_loop(0, lag, top_only, 0)
    lax.fori_loop(lag, nc, both, 0)
    rs_start(1)
    put(xtop, xtop_h, 0).start()
    put(skip, skip_h, 1).start()
    lax.fori_loop(nc - lag, nc, low_only, 0)
    rs_start(0)
    z_start(1)
    z_start(0)
    ag_start(1)
    lax.fori_loop(0, nc, finish, 0)
    put(ginp, ginp_h, 2).start()
    ag_start(0)
    ag_finish(1)
    ag_finish(0)
    put(gcbias, gcbias_h, 3).start()
    put(gobias, gobias_h, 4).start()

    put(xtop, xtop_h, 0).wait()
    put(skip, skip_h, 1).wait()
    put(ginp, ginp_h, 2).wait()
    put(gcbias, gcbias_h, 3).wait()
    put(gobias, gobias_h, 4).wait()
    for l in range(2):
        put(total.at[l, 0:g2], gconv_h.at[l], 5 + l).wait()
        put(total.at[l, g2 : g2 + po], gout_h.at[l], 7 + l).wait()

    def sent(i, carry):
        @pl.when(zi < ntm - 1)
        def _():
            sig_copy(i).wait_send()

        @pl.when(zi < ntm - 2)
        def _():
            x_copy(i).wait_send()

        @pl.when(zi >= 2)
        def _():
            d1_copy(i).wait_send()

        @pl.when(zi >= 1)
        def _():
            d0_copy(i).wait_send()

        return carry

    lax.fori_loop(0, nc, sent, 0)
    for l in range(2):
        each(ncor, lambda j: rs_copy(l, j).wait_send())
        each(ntm, lambda j: z_copy(l, j).wait_send())
        each(ncor, lambda j: ag_copy(l, j).wait_send())


def deliver(*refs):
    sems = refs[14]
    moves = [pltpu.make_async_copy(refs[k], refs[7 + k], sems.at[k]) for k in range(7)]
    for m in moves:
        m.start()
    for m in moves:
        m.wait()


def on_device(sig, w, wb, p, pb, ct, cs):
    ncor = lax.axis_size("corner")
    ntm = lax.axis_size("tm")
    _, r, time = sig.shape
    _, g2, _ = w.shape
    _, po, g = p.shape
    t = CHUNK
    nc = time // t
    used = g2 + po + g2 // 128 + 1
    rows = -(-used // (ncor * 8)) * 8
    count = sig.shape[0] * ncor * time * ntm
    cfg = (ncor, ntm, nc, t, rows, 1.0 / math.sqrt(count))
    hbm = pl.BlockSpec(memory_space=pltpu.HBM)
    room = 62 * 1024 * 1024
    dma = pltpu.SemaphoreType.DMA
    field = pltpu.VMEM((nc, r, t), BF16)
    field32 = pltpu.VMEM((nc, r, t), F32)
    flops = 2 * 2 * time * 3 * (g2 * 2 * r + po * g)
    args = (sig, w, wb, p, pb, ct, cs)
    outs = pl.pallas_call(
        functools.partial(kernel, cfg),
        out_shape=(
            jax.ShapeDtypeStruct(sig.shape, BF16),
            jax.ShapeDtypeStruct(sig.shape, BF16),
            jax.ShapeDtypeStruct(sig.shape, BF16),
            jax.ShapeDtypeStruct(w.shape, F32),
            jax.ShapeDtypeStruct(wb.shape, F32),
            jax.ShapeDtypeStruct(p.shape, F32),
            jax.ShapeDtypeStruct(pb.shape, F32),
        ),
        in_specs=[hbm] * 7,
        out_specs=[hbm] * 7,
        scratch_shapes=[pltpu.VMEM(a.shape, a.dtype) for a in args]
        + [
            dma((7,)),
            pltpu.VMEM(sig.shape, BF16),
            pltpu.VMEM(sig.shape, BF16),
            pltpu.VMEM(sig.shape, BF16),
            pltpu.VMEM(wb.shape, F32),
            pltpu.VMEM(pb.shape, F32),
            dma((9,)),
            field,
            field,
            field,
            field,
            field,
            field,
            field,
            pltpu.VMEM((nc, g, t), F32),
            pltpu.VMEM((nc, g, t), F32),
            pltpu.VMEM((nc, g, t), BF16),
            field32,
            field32,
            field32,
            pltpu.VMEM((2, w.shape[2], g2), BF16),
            pltpu.VMEM((2, g, po), BF16),
            pltpu.VMEM((2, g2, 128), F32),
            pltpu.VMEM((2, po, 128), F32),
            pltpu.VMEM((2, g2, 256), F32),
            pltpu.VMEM((2, po, 256), F32),
            pltpu.VMEM((2, ncor * rows, 128), F32),
            pltpu.VMEM((2, ncor - 1, rows, 128), F32),
            pltpu.VMEM((2, ntm, rows, 128), F32),
            pltpu.VMEM((2, ncor * rows, 128), F32),
        ]
        + [dma((nc,))] * 8
        + [dma((2, ncor - 1))] * 2
        + [dma((2, ntm - 1))] * 2
        + [dma((2, ncor - 1))] * 2,
        compiler_params=pltpu.CompilerParams(
            collective_id=0, has_side_effects=True, vmem_limit_bytes=room
        ),
        cost_estimate=pl.CostEstimate(
            flops=flops, bytes_accessed=6 * sig.size * 2, transcendentals=2 * g2 * time
        ),
    )(*args)
    return pl.pallas_call(
        deliver,
        out_shape=tuple(jax.ShapeDtypeStruct(a.shape, a.dtype) for a in outs),
        in_specs=[hbm] * 7,
        out_specs=[hbm] * 7,
        scratch_shapes=[dma((7,))],
        compiler_params=pltpu.CompilerParams(vmem_limit_bytes=room),
    )(*outs)


def solution(mesh):
    field = P("corner", None, "tm")
    return jax.shard_map(
        on_device,
        mesh=mesh,
        in_specs=(field, P(), P(), P(), P(), field, field),
        out_specs=(field, field, field, P(), P(), P(), P()),
        check_vma=False,
    )
```

```python
import functools
import math

import jax
import jax.numpy as jnp
from jax import lax
from jax.experimental import pallas as pl
from jax.experimental.pallas import tpu as pltpu
from jax.sharding import PartitionSpec as P

MESH = pl.DeviceIdType.MESH
F32 = jnp.float32
BF16 = jnp.bfloat16
CHUNK = 512
LAG = 2


def dot(a, b):
    return jnp.dot(a, b, preferred_element_type=F32)


def dot_nt(a, b):
    return lax.dot_general(a, b, (((1,), (1,)), ((), ())), preferred_element_type=F32)


def kernel(
    cfg,
    sig_h,
    w_h,
    wb_h,
    p_h,
    pb_h,
    ct_h,
    cs_h,
    xtop_h,
    skip_h,
    ginp_h,
    gconv_h,
    gcbias_h,
    gout_h,
    gobias_h,
    sig,
    w,
    wb,
    p,
    pb,
    ct,
    cs,
    in_s,
    xtop,
    skip,
    ginp,
    gconv,
    gcbias,
    gout,
    gobias,
    out_s,
    tap0,
    xmid,
    tap1,
    gdel1,
    d1,
    gdel0,
    d0,
    df0,
    dg0,
    z0,
    skip0,
    res1,
    res0,
    wt,
    pt,
    wbc,
    pbc,
    accw,
    accp,
    bias,
    part,
    rs_buf,
    z_buf,
    total,
    sig_s,
    sig_r,
    x_s,
    x_r,
    d1_s,
    d1_r,
    d0_s,
    d0_r,
    rs_s,
    rs_r,
    z_s,
    z_r,
    ag_s,
    ag_r,
):
    ncor, ntm, nc, t, rows, scale = cfg
    lag = min(LAG, nc)
    r = sig.shape[1]
    g = p.shape[2]
    g2 = w.shape[1]
    po = p.shape[1]
    me = lax.axis_index("corner")
    zi = lax.axis_index("tm")

    def cols(i):
        return pl.ds(pl.multiple_of(i * t, t), t)

    def shift_copy(src, dst, ssem, rsem, i, distance):
        return pltpu.make_async_remote_copy(
            src_ref=src,
            dst_ref=dst.at[i],
            send_sem=ssem.at[i],
            recv_sem=rsem.at[i],
            device_id={"tm": lax.rem(zi + distance + ntm, ntm)},
            device_id_type=MESH,
        )

    def sig_copy(i):
        return shift_copy(sig.at[0, :, cols(i)], tap0, sig_s, sig_r, i, 1)

    def x_copy(i):
        return shift_copy(xmid.at[i], tap1, x_s, x_r, i, 2)

    def d1_copy(i):
        return shift_copy(gdel1.at[i], d1, d1_s, d1_r, i, -2)

    def d0_copy(i):
        return shift_copy(gdel0.at[i], d0, d0_s, d0_r, i, -1)

    moves = [
        pltpu.make_async_copy(a, b, in_s.at[k])
        for k, (a, b) in enumerate(
            ((sig_h, sig), (w_h, w), (wb_h, wb), (p_h, p), (pb_h, pb), (ct_h, ct), (cs_h, cs))
        )
    ]
    for m in moves:
        m.start()

    barrier = pltpu.get_barrier_semaphore()

    def greet_corner(j, carry):
        pl.semaphore_signal(
            barrier, inc=1, device_id={"corner": lax.rem(me + j, ncor)}, device_id_type=MESH
        )
        return carry

    def greet_tm(j, carry):
        pl.semaphore_signal(
            barrier, inc=1, device_id={"tm": lax.rem(zi + j, ntm)}, device_id_type=MESH
        )
        return carry

    lax.fori_loop(1, ncor, greet_corner, 0)
    lax.fori_loop(1, ntm, greet_tm, 0)

    for m in moves:
        m.wait()
    for l in range(2):
        wt[l] = w[l].astype(F32).T.astype(BF16)
        pt[l] = p[l].astype(F32).T.astype(BF16)
        wbc[l] = jnp.broadcast_to(wb[l : l + 1, :], (128, g2)).T
        pbc[l] = jnp.broadcast_to(pb[l : l + 1, :], (128, po)).T
    accw[...] = jnp.zeros_like(accw)
    accp[...] = jnp.zeros_like(accp)
    part[...] = jnp.zeros_like(part)
    bias[...] = jnp.zeros_like(bias)

    @pl.when(zi < 1)
    def _():
        tap0[...] = jnp.zeros_like(tap0)

    @pl.when(zi < 2)
    def _():
        tap1[...] = jnp.zeros_like(tap1)

    @pl.when(zi >= ntm - 2)
    def _():
        d1[...] = jnp.zeros_like(d1)

    @pl.when(zi >= ntm - 1)
    def _():
        d0[...] = jnp.zeros_like(d0)

    pl.semaphore_wait(barrier, ncor - 1 + ntm - 1)

    @pl.when(zi < ntm - 1)
    def _():
        def send(i, carry):
            sig_copy(i).start()
            return carry

        lax.fori_loop(0, nc, send, 0)

    ones = jnp.ones((128, t), BF16)

    def wide(ref, l):
        return jnp.concatenate([ref[l]] * (t // 128), axis=1)

    def gates(l, stacked):
        pre = dot(w[l], stacked) + wide(wbc, l)
        th = jnp.tanh(pre[:g])
        sg = 0.5 * jnp.tanh(0.5 * pre[g:]) + 0.5
        z = th * sg
        zb = z.astype(BF16)
        mixed = dot(p[l], zb) + wide(pbc, l)
        return sg - z * th, z - z * sg, zb, mixed

    def accumulate(l, gpre, stacked, u, zb):
        accw[l] += dot_nt(gpre, jnp.concatenate([stacked, ones], axis=0))
        accp[l] += dot_nt(u, jnp.concatenate([zb, ones], axis=0))

    def forward_low(i, carry):
        @pl.when(zi >= 1)
        def _():
            sig_copy(i).wait_recv()

        a = sig[0, :, cols(i)]
        df, dg, zb, mixed = gates(0, jnp.concatenate([tap0[i], a], axis=0))
        xmid[i] = (a.astype(F32) + mixed[:r]).astype(BF16)
        df0[i] = df
        dg0[i] = dg
        z0[i] = zb
        skip0[i] = mixed[r:]

        @pl.when(zi < ntm - 2)
        def _():
            x_copy(i).start()

        return carry

    def wait_x(i):
        @pl.when(zi >= 2)
        def _():
            x_copy(i).wait_recv()

    def send_d1(i):
        @pl.when(zi >= 2)
        def _():
            d1_copy(i).start()

    def wait_d1(i):
        @pl.when(zi < ntm - 2)
        def _():
            d1_copy(i).wait_recv()

    def send_d0(i):
        @pl.when(zi >= 1)
        def _():
            d0_copy(i).start()

    def top(i):
        a = xmid[i]
        stacked = jnp.concatenate([tap1[i], a], axis=0)
        df, dg, zb, mixed = gates(1, stacked)
        c = ct[0, :, cols(i)]
        u = jnp.concatenate([c, cs[0, :, cols(i)]], axis=0)
        gz = dot(pt[1], u)
        gpre = jnp.concatenate([gz * df, gz * dg], axis=0).astype(BF16)
        gin = dot(wt[1], gpre)
        gdel1[i] = gin[:r].astype(BF16)
        res1[i] = c.astype(F32) + gin[r:]
        xtop[0, :, cols(i)] = (a.astype(F32) + mixed[:r]).astype(BF16)
        skip[0, :, cols(i)] = (skip0[i] + mixed[r:]).astype(BF16)
        accumulate(1, gpre, stacked, u, zb)

    def low(i):
        gm = (res1[i] + d1[i].astype(F32)).astype(BF16)
        u = jnp.concatenate([gm, cs[0, :, cols(i)]], axis=0)
        gz = dot(pt[0], u)
        gpre = jnp.concatenate([gz * df0[i], gz * dg0[i]], axis=0).astype(BF16)
        gin = dot(wt[0], gpre)
        gdel0[i] = gin[:r].astype(BF16)
        res0[i] = gm.astype(F32) + gin[r:]
        stacked = jnp.concatenate([tap0[i], sig[0, :, cols(i)]], axis=0)
        accumulate(0, gpre, stacked, u, z0[i])

    def top_only(i, carry):
        wait_x(i)
        top(i)
        send_d1(i)
        return carry

    def both(i, carry):
        wait_x(i)
        wait_d1(i - lag)
        low(i - lag)
        top(i)
        send_d1(i)
        send_d0(i - lag)
        return carry

    def low_only(i, carry):
        wait_d1(i)
        low(i)
        send_d0(i)
        return carry

    def finish(i, carry):
        @pl.when(zi < ntm - 1)
        def _():
            d0_copy(i).wait_recv()

        ginp[0, :, cols(i)] = (res0[i] + d0[i].astype(F32)).astype(BF16)
        return carry

    def shard(k):
        return pl.ds(pl.multiple_of(k * rows, 16), rows)

    def reduce_copy(src, dst, ssem, rsem, j, axis, to):
        return pltpu.make_async_remote_copy(
            src_ref=src,
            dst_ref=dst,
            send_sem=ssem.at[j - 1],
            recv_sem=rsem.at[j - 1],
            device_id={axis: to},
            device_id_type=MESH,
        )

    def rs_copy(j):
        to = lax.rem(me + j, ncor)
        return reduce_copy(part.at[shard(to)], rs_buf.at[j - 1], rs_s, rs_r, j, "corner", to)

    def z_copy(j, slot):
        to = lax.rem(zi + j, ntm)
        return reduce_copy(z_buf.at[zi], z_buf.at[slot], z_s, z_r, j, "tm", to)

    def ag_copy(j, owner):
        to = lax.rem(me + j, ncor)
        return reduce_copy(
            total.at[shard(me)], total.at[shard(owner)], ag_s, ag_r, j, "corner", to
        )

    def z_from(j):
        return lax.rem(zi - j + ntm, ntm)

    def ag_from(j):
        return lax.rem(me - j + ncor, ncor)

    def put(src, dst, k):
        return pltpu.make_async_copy(src, dst, out_s.at[k])

    def each(n, body):
        def step(j, carry):
            body(j)
            return carry

        lax.fori_loop(1, n, step, 0)

    mats = g2 + po
    cuts = g2 // 128

    def fill(l):
        part[l * mats : l * mats + g2] = accw[l, :, 0:128].astype(BF16)
        part[l * mats + g2 : (l + 1) * mats] = accp[l, :, 0:128].astype(BF16)
        brow = accw[l, :, 128:256].T
        for k in range(cuts):
            at = l * (cuts + 1) + k
            bias[at : at + 1] = brow[0:1, k * 128 : (k + 1) * 128]
        at = l * (cuts + 1) + cuts
        bias[at : at + 1] = accp[l, :, 128:256].T[0:1, :]

    def rs_start():
        part[2 * mats : 2 * mats + 16] = bias[...].astype(BF16)
        each(ncor, lambda j: rs_copy(j).start())

    def z_start():
        each(ncor, lambda j: rs_copy(j).wait_recv())
        s = part[shard(me)].astype(F32)
        for j in range(ncor - 1):
            s = s + rs_buf[j].astype(F32)
        z_buf[zi] = s.astype(BF16)
        each(ntm, lambda j: z_copy(j, zi).start())

    def ag_start():
        each(ntm, lambda j: z_copy(j, z_from(j)).wait_recv())
        s = z_buf[0].astype(F32)
        for j in range(1, ntm):
            s = s + z_buf[j].astype(F32)
        total[shard(me)] = (s * scale).astype(BF16)
        each(ncor, lambda j: ag_copy(j, me).start())

    def ag_finish():
        each(ncor, lambda j: ag_copy(j, ag_from(j)).wait_recv())
        tail = total[2 * mats : 2 * mats + 16].astype(F32)
        for l in range(2):
            gconv[l] = total[l * mats : l * mats + g2].astype(F32)
            gout[l] = total[l * mats + g2 : (l + 1) * mats].astype(F32)
            for k in range(cuts):
                at = l * (cuts + 1) + k
                gcbias[l : l + 1, k * 128 : (k + 1) * 128] = tail[at : at + 1]
            at = l * (cuts + 1) + cuts
            gobias[l : l + 1, :] = tail[at : at + 1]

    lax.fori_loop(0, nc, forward_low, 0)
    lax.fori_loop(0, lag, top_only, 0)
    lax.fori_loop(lag, nc, both, 0)
    put(xtop, xtop_h, 0).start()
    put(skip, skip_h, 1).start()
    fill(1)
    lax.fori_loop(nc - lag, nc, low_only, 0)
    fill(0)
    rs_start()
    z_start()
    lax.fori_loop(0, nc, finish, 0)
    put(ginp, ginp_h, 2).start()
    ag_start()
    ag_finish()
    for k, (a, b) in enumerate(
        ((gconv, gconv_h), (gcbias, gcbias_h), (gout, gout_h), (gobias, gobias_h))
    ):
        put(a, b, 3 + k).start()

    def sent(i, carry):
        @pl.when(zi < ntm - 1)
        def _():
            sig_copy(i).wait_send()

        @pl.when(zi < ntm - 2)
        def _():
            x_copy(i).wait_send()

        @pl.when(zi >= 2)
        def _():
            d1_copy(i).wait_send()

        @pl.when(zi >= 1)
        def _():
            d0_copy(i).wait_send()

        return carry

    lax.fori_loop(0, nc, sent, 0)
    each(ncor, lambda j: rs_copy(j).wait_send())
    each(ntm, lambda j: z_copy(j, zi).wait_send())
    each(ncor, lambda j: ag_copy(j, me).wait_send())
    for k, (a, b) in enumerate(
        (
            (xtop, xtop_h),
            (skip, skip_h),
            (ginp, ginp_h),
            (gconv, gconv_h),
            (gcbias, gcbias_h),
            (gout, gout_h),
            (gobias, gobias_h),
        )
    ):
        put(a, b, k).wait()


def deliver(*refs):
    held, sems = refs[14:21], refs[21]
    ins = [pltpu.make_async_copy(refs[k], held[k], sems.at[0, k]) for k in range(7)]
    outs = [pltpu.make_async_copy(held[k], refs[7 + k], sems.at[1, k]) for k in range(7)]
    for m in ins:
        m.start()
    for a, b in zip(ins, outs):
        a.wait()
        b.start()
    for b in outs:
        b.wait()


def on_device(sig, w, wb, p, pb, ct, cs):
    ncor = lax.axis_size("corner")
    ntm = lax.axis_size("tm")
    _, r, time = sig.shape
    _, g2, _ = w.shape
    _, po, g = p.shape
    t = CHUNK
    nc = time // t
    used = 2 * (g2 + po) + 16
    rows = -(-used // (ncor * 16)) * 16
    count = sig.shape[0] * ncor * time * ntm
    cfg = (ncor, ntm, nc, t, rows, 1.0 / math.sqrt(count))
    hbm = pl.BlockSpec(memory_space=pltpu.HBM)
    room = 62 * 1024 * 1024
    dma = pltpu.SemaphoreType.DMA
    field = pltpu.VMEM((nc, r, t), BF16)
    field32 = pltpu.VMEM((nc, r, t), F32)
    flops = 2 * 2 * time * 3 * (g2 * 2 * r + po * g)
    args = (sig, w, wb, p, pb, ct, cs)
    outs = pl.pallas_call(
        functools.partial(kernel, cfg),
        out_shape=(
            jax.ShapeDtypeStruct(sig.shape, BF16),
            jax.ShapeDtypeStruct(sig.shape, BF16),
            jax.ShapeDtypeStruct(sig.shape, BF16),
            jax.ShapeDtypeStruct(w.shape, F32),
            jax.ShapeDtypeStruct(wb.shape, F32),
            jax.ShapeDtypeStruct(p.shape, F32),
            jax.ShapeDtypeStruct(pb.shape, F32),
        ),
        in_specs=[hbm] * 7,
        out_specs=[hbm] * 7,
        scratch_shapes=[pltpu.VMEM(a.shape, a.dtype) for a in args]
        + [
            dma((7,)),
            pltpu.VMEM(sig.shape, BF16),
            pltpu.VMEM(sig.shape, BF16),
            pltpu.VMEM(sig.shape, BF16),
            pltpu.VMEM(w.shape, F32),
            pltpu.VMEM(wb.shape, F32),
            pltpu.VMEM(p.shape, F32),
            pltpu.VMEM(pb.shape, F32),
            dma((7,)),
            field,
            field,
            field,
            field,
            field,
            field,
            field,
            pltpu.VMEM((nc, g, t), F32),
            pltpu.VMEM((nc, g, t), F32),
            pltpu.VMEM((nc, g, t), BF16),
            field32,
            field32,
            field32,
            pltpu.VMEM((2, w.shape[2], g2), BF16),
            pltpu.VMEM((2, g, po), BF16),
            pltpu.VMEM((2, g2, 128), F32),
            pltpu.VMEM((2, po, 128), F32),
            pltpu.VMEM((2, g2, 256), F32),
            pltpu.VMEM((2, po, 256), F32),
            pltpu.VMEM((16, 128), F32),
            pltpu.VMEM((ncor * rows, 128), BF16),
            pltpu.VMEM((ncor - 1, rows, 128), BF16),
            pltpu.VMEM((ntm, rows, 128), BF16),
            pltpu.VMEM((ncor * rows, 128), BF16),
        ]
        + [dma((nc,))] * 8
        + [dma((ncor - 1,))] * 2
        + [dma((ntm - 1,))] * 2
        + [dma((ncor - 1,))] * 2,
        compiler_params=pltpu.CompilerParams(
            collective_id=0, has_side_effects=True, vmem_limit_bytes=room
        ),
        cost_estimate=pl.CostEstimate(
            flops=flops, bytes_accessed=6 * sig.size * 2, transcendentals=2 * g2 * time
        ),
    )(*args)
    return pl.pallas_call(
        deliver,
        out_shape=tuple(jax.ShapeDtypeStruct(a.shape, a.dtype) for a in outs),
        in_specs=[hbm] * 7,
        out_specs=[hbm] * 7,
        scratch_shapes=[pltpu.VMEM(a.shape, a.dtype) for a in outs] + [dma((2, 7))],
        compiler_params=pltpu.CompilerParams(vmem_limit_bytes=room),
    )(*outs)


def solution(mesh):
    field = P("corner", None, "tm")
    return jax.shard_map(
        on_device,
        mesh=mesh,
        in_specs=(field, P(), P(), P(), P(), field, field),
        out_specs=(field, field, field, P(), P(), P(), P()),
        check_vma=False,
    )
```

```python
import functools
import math

import jax
import jax.numpy as jnp
from jax import lax
from jax.experimental import pallas as pl
from jax.experimental.pallas import tpu as pltpu
from jax.sharding import PartitionSpec as P

MESH = pl.DeviceIdType.MESH
F32 = jnp.float32
BF16 = jnp.bfloat16
CHUNK = 512
LAG_TOP = 1
LAG_LOW = 3


def dot(a, b):
    return jnp.dot(a, b, preferred_element_type=F32)


def dot_nt(a, b):
    return lax.dot_general(a, b, (((1,), (1,)), ((), ())), preferred_element_type=F32)


def kernel(
    cfg,
    sig_h,
    w_h,
    wb_h,
    p_h,
    pb_h,
    ct_h,
    cs_h,
    xtop_h,
    skip_h,
    ginp_h,
    gconv_h,
    gcbias_h,
    gout_h,
    gobias_h,
    sig,
    w,
    wb,
    p,
    pb,
    ct,
    cs,
    in_s,
    xtop,
    skip,
    ginp,
    gconv,
    gcbias,
    gout,
    gobias,
    out_s,
    tap0,
    xmid,
    tap1,
    gdel1,
    d1,
    gdel0,
    d0,
    df0,
    dg0,
    z0,
    skip0,
    res1,
    res0,
    wt,
    pt,
    wbc,
    pbc,
    accw,
    accp,
    accb,
    bias,
    part,
    rs_buf,
    z_buf,
    total,
    sig_s,
    sig_r,
    x_s,
    x_r,
    d1_s,
    d1_r,
    d0_s,
    d0_r,
    rs_s,
    rs_r,
    z_s,
    z_r,
    ag_s,
    ag_r,
):
    ncor, ntm, nc, t, rows, scale = cfg
    r = sig.shape[1]
    g = p.shape[2]
    g2 = w.shape[1]
    po = p.shape[1]
    me = lax.axis_index("corner")
    zi = lax.axis_index("tm")

    def cols(i):
        return pl.ds(i * t if isinstance(i, int) else pl.multiple_of(i * t, t), t)

    def shift_copy(src, dst, ssem, rsem, i, distance):
        return pltpu.make_async_remote_copy(
            src_ref=src,
            dst_ref=dst.at[i],
            send_sem=ssem.at[i],
            recv_sem=rsem.at[i],
            device_id={"tm": lax.rem(zi + distance + ntm, ntm)},
            device_id_type=MESH,
        )

    def sig_copy(i):
        return shift_copy(sig.at[0, :, cols(i)], tap0, sig_s, sig_r, i, 1)

    def x_copy(i):
        return shift_copy(xmid.at[i], tap1, x_s, x_r, i, 2)

    def d1_copy(i):
        return shift_copy(gdel1.at[i], d1, d1_s, d1_r, i, -2)

    def d0_copy(i):
        return shift_copy(gdel0.at[i], d0, d0_s, d0_r, i, -1)

    moves = [
        pltpu.make_async_copy(a, b, in_s.at[k])
        for k, (a, b) in enumerate(
            ((sig_h, sig), (w_h, w), (wb_h, wb), (p_h, p), (pb_h, pb), (ct_h, ct), (cs_h, cs))
        )
    ]
    for m in moves:
        m.start()

    barrier = pltpu.get_barrier_semaphore()

    def greet_corner(j, carry):
        pl.semaphore_signal(
            barrier, inc=1, device_id={"corner": lax.rem(me + j, ncor)}, device_id_type=MESH
        )
        return carry

    def greet_tm(j, carry):
        pl.semaphore_signal(
            barrier, inc=1, device_id={"tm": lax.rem(zi + j, ntm)}, device_id_type=MESH
        )
        return carry

    lax.fori_loop(1, ncor, greet_corner, 0)
    lax.fori_loop(1, ntm, greet_tm, 0)

    for m in moves:
        m.wait()
    for l in range(2):
        wt[l] = w[l].astype(F32).T.astype(BF16)
        pt[l] = p[l].astype(F32).T.astype(BF16)
        wbc[l] = jnp.broadcast_to(wb[l : l + 1, :], (128, g2)).T
        pbc[l] = jnp.broadcast_to(pb[l : l + 1, :], (128, po)).T
    accw[...] = jnp.zeros_like(accw)
    accp[...] = jnp.zeros_like(accp)
    accb[...] = jnp.zeros_like(accb)
    part[...] = jnp.zeros_like(part)
    bias[...] = jnp.zeros_like(bias)

    @pl.when(zi < 1)
    def _():
        tap0[...] = jnp.zeros_like(tap0)

    @pl.when(zi < 2)
    def _():
        tap1[...] = jnp.zeros_like(tap1)

    @pl.when(zi >= ntm - 2)
    def _():
        d1[...] = jnp.zeros_like(d1)

    @pl.when(zi >= ntm - 1)
    def _():
        d0[...] = jnp.zeros_like(d0)

    pl.semaphore_wait(barrier, ncor - 1 + ntm - 1)

    @pl.when(zi < ntm - 1)
    def _():
        def send(i, carry):
            sig_copy(i).start()
            return carry

        lax.fori_loop(0, nc, send, 0)

    def fold(v):
        v = v.astype(F32)
        s = v[:, 0:128]
        for k in range(1, t // 128):
            s = s + v[:, k * 128 : (k + 1) * 128]
        return s

    def wide(ref, l):
        return jnp.concatenate([ref[l]] * (t // 128), axis=1)

    def gates(l, stacked):
        pre = dot(w[l], stacked) + wide(wbc, l)
        th = jnp.tanh(pre[:g])
        sg = 0.5 * jnp.tanh(0.5 * pre[g:]) + 0.5
        z = th * sg
        zb = z.astype(BF16)
        mixed = dot(p[l], zb) + wide(pbc, l)
        return sg - z * th, z - z * sg, zb, mixed

    def accumulate(l, gpre, stacked, u, zb):
        accw[l] += dot_nt(gpre, stacked)
        accp[l] += dot_nt(u, zb)
        accb[l, 0:g2] += fold(gpre)
        accb[l, g2 : g2 + po] += fold(u)

    def wait_sig(i):
        @pl.when(zi >= 1)
        def _():
            sig_copy(i).wait_recv()

    def send_x(i):
        @pl.when(zi < ntm - 2)
        def _():
            x_copy(i).start()

    def forward_low(i):
        a = sig[0, :, cols(i)]
        df, dg, zb, mixed = gates(0, jnp.concatenate([tap0[i], a], axis=0))
        xmid[i] = (a.astype(F32) + mixed[:r]).astype(BF16)
        df0[i] = df
        dg0[i] = dg
        z0[i] = zb
        skip0[i] = mixed[r:]

    def wait_x(i):
        @pl.when(zi >= 2)
        def _():
            x_copy(i).wait_recv()

    def send_d1(i):
        @pl.when(zi >= 2)
        def _():
            d1_copy(i).start()

    def wait_d1(i):
        @pl.when(zi < ntm - 2)
        def _():
            d1_copy(i).wait_recv()

    def send_d0(i):
        @pl.when(zi >= 1)
        def _():
            d0_copy(i).start()

    def top(i):
        a = xmid[i]
        stacked = jnp.concatenate([tap1[i], a], axis=0)
        df, dg, zb, mixed = gates(1, stacked)
        c = ct[0, :, cols(i)]
        u = jnp.concatenate([c, cs[0, :, cols(i)]], axis=0)
        gz = dot(pt[1], u)
        gpre = jnp.concatenate([gz * df, gz * dg], axis=0).astype(BF16)
        gin = dot(wt[1], gpre)
        gdel1[i] = gin[:r].astype(BF16)
        res1[i] = c.astype(F32) + gin[r:]
        xtop[0, :, cols(i)] = (a.astype(F32) + mixed[:r]).astype(BF16)
        skip[0, :, cols(i)] = (skip0[i] + mixed[r:]).astype(BF16)
        accumulate(1, gpre, stacked, u, zb)

    def low(i):
        gm = (res1[i] + d1[i].astype(F32)).astype(BF16)
        u = jnp.concatenate([gm, cs[0, :, cols(i)]], axis=0)
        gz = dot(pt[0], u)
        gpre = jnp.concatenate([gz * df0[i], gz * dg0[i]], axis=0).astype(BF16)
        gin = dot(wt[0], gpre)
        gdel0[i] = gin[:r].astype(BF16)
        res0[i] = gm.astype(F32) + gin[r:]
        stacked = jnp.concatenate([tap0[i], sig[0, :, cols(i)]], axis=0)
        accumulate(0, gpre, stacked, u, z0[i])

    def step(i, first, second, third):
        j, k = i - LAG_TOP, i - LAG_LOW
        if first:
            wait_sig(i)
        if second:
            wait_x(j)
        if third:
            wait_d1(k)
        if third:
            low(k)
        if first:
            forward_low(i)
        if second:
            top(j)
        if first:
            send_x(i)
        if second:
            send_d1(j)
        if third:
            send_d0(k)

    def finish(i, carry):
        @pl.when(zi < ntm - 1)
        def _():
            d0_copy(i).wait_recv()

        ginp[0, :, cols(i)] = (res0[i] + d0[i].astype(F32)).astype(BF16)
        return carry

    def shard(k):
        return pl.ds(pl.multiple_of(k * rows, 16), rows)

    def reduce_copy(src, dst, ssem, rsem, j, axis, to):
        return pltpu.make_async_remote_copy(
            src_ref=src,
            dst_ref=dst,
            send_sem=ssem.at[j - 1],
            recv_sem=rsem.at[j - 1],
            device_id={axis: to},
            device_id_type=MESH,
        )

    def rs_copy(j):
        to = lax.rem(me + j, ncor)
        return reduce_copy(part.at[shard(to)], rs_buf.at[j - 1], rs_s, rs_r, j, "corner", to)

    def z_copy(j, slot):
        to = lax.rem(zi + j, ntm)
        return reduce_copy(z_buf.at[zi], z_buf.at[slot], z_s, z_r, j, "tm", to)

    def ag_copy(j, owner):
        to = lax.rem(me + j, ncor)
        return reduce_copy(
            total.at[shard(me)], total.at[shard(owner)], ag_s, ag_r, j, "corner", to
        )

    def z_from(j):
        return lax.rem(zi - j + ntm, ntm)

    def ag_from(j):
        return lax.rem(me - j + ncor, ncor)

    def put(src, dst, k):
        return pltpu.make_async_copy(src, dst, out_s.at[k])

    def each(n, body):
        def step(j, carry):
            body(j)
            return carry

        lax.fori_loop(1, n, step, 0)

    mats = g2 + po
    cuts = g2 // 128

    def fill(l):
        part[l * mats : l * mats + g2] = accw[l].astype(BF16)
        part[l * mats + g2 : (l + 1) * mats] = accp[l].astype(BF16)
        brow = jnp.sum(accb[l].T, axis=0, keepdims=True)
        for k in range(cuts + 1):
            at = l * (cuts + 1) + k
            bias[at : at + 1] = brow[:, k * 128 : (k + 1) * 128]

    def rs_start():
        part[2 * mats : 2 * mats + 16] = bias[...].astype(BF16)
        each(ncor, lambda j: rs_copy(j).start())

    def z_start():
        each(ncor, lambda j: rs_copy(j).wait_recv())
        s = part[shard(me)].astype(F32)
        for j in range(ncor - 1):
            s = s + rs_buf[j].astype(F32)
        z_buf[zi] = s.astype(BF16)
        each(ntm, lambda j: z_copy(j, zi).start())

    def ag_start():
        each(ntm, lambda j: z_copy(j, z_from(j)).wait_recv())
        s = z_buf[0].astype(F32)
        for j in range(1, ntm):
            s = s + z_buf[j].astype(F32)
        total[shard(me)] = (s * scale).astype(BF16)
        each(ncor, lambda j: ag_copy(j, me).start())

    def ag_finish():
        each(ncor, lambda j: ag_copy(j, ag_from(j)).wait_recv())
        tail = total[2 * mats : 2 * mats + 16].astype(F32)
        for l in range(2):
            gconv[l] = total[l * mats : l * mats + g2].astype(F32)
            gout[l] = total[l * mats + g2 : (l + 1) * mats].astype(F32)
            for k in range(cuts):
                at = l * (cuts + 1) + k
                gcbias[l : l + 1, k * 128 : (k + 1) * 128] = tail[at : at + 1]
            at = l * (cuts + 1) + cuts
            gobias[l : l + 1, :] = tail[at : at + 1]

    def full(i, carry):
        step(i, True, True, True)
        return carry

    for i in range(LAG_LOW):
        step(i, True, i >= LAG_TOP, False)
    lax.fori_loop(LAG_LOW, nc, full, 0)
    for i in range(nc, nc + LAG_TOP):
        step(i, False, True, True)
    put(xtop, xtop_h, 0).start()
    put(skip, skip_h, 1).start()
    fill(1)
    for i in range(nc + LAG_TOP, nc + LAG_LOW):
        step(i, False, False, True)
    fill(0)
    rs_start()
    z_start()
    lax.fori_loop(0, nc, finish, 0)
    put(ginp, ginp_h, 2).start()
    ag_start()
    ag_finish()
    for k, (a, b) in enumerate(
        ((gconv, gconv_h), (gcbias, gcbias_h), (gout, gout_h), (gobias, gobias_h))
    ):
        put(a, b, 3 + k).start()

    def sent(i, carry):
        @pl.when(zi < ntm - 1)
        def _():
            sig_copy(i).wait_send()

        @pl.when(zi < ntm - 2)
        def _():
            x_copy(i).wait_send()

        @pl.when(zi >= 2)
        def _():
            d1_copy(i).wait_send()

        @pl.when(zi >= 1)
        def _():
            d0_copy(i).wait_send()

        return carry

    lax.fori_loop(0, nc, sent, 0)
    each(ncor, lambda j: rs_copy(j).wait_send())
    each(ntm, lambda j: z_copy(j, zi).wait_send())
    each(ncor, lambda j: ag_copy(j, me).wait_send())
    for k, (a, b) in enumerate(
        (
            (xtop, xtop_h),
            (skip, skip_h),
            (ginp, ginp_h),
            (gconv, gconv_h),
            (gcbias, gcbias_h),
            (gout, gout_h),
            (gobias, gobias_h),
        )
    ):
        put(a, b, k).wait()


def deliver(*refs):
    held, sems = refs[14:21], refs[21]
    ins = [pltpu.make_async_copy(refs[k], held[k], sems.at[0, k]) for k in range(7)]
    outs = [pltpu.make_async_copy(held[k], refs[7 + k], sems.at[1, k]) for k in range(7)]
    for m in ins:
        m.start()
    for a, b in zip(ins, outs):
        a.wait()
        b.start()
    for b in outs:
        b.wait()


def on_device(sig, w, wb, p, pb, ct, cs):
    ncor = lax.axis_size("corner")
    ntm = lax.axis_size("tm")
    _, r, time = sig.shape
    _, g2, _ = w.shape
    _, po, g = p.shape
    t = CHUNK
    nc = time // t
    used = 2 * (g2 + po) + 16
    rows = -(-used // (ncor * 16)) * 16
    count = sig.shape[0] * ncor * time * ntm
    cfg = (ncor, ntm, nc, t, rows, 1.0 / math.sqrt(count))
    hbm = pl.BlockSpec(memory_space=pltpu.HBM)
    room = 62 * 1024 * 1024
    dma = pltpu.SemaphoreType.DMA
    field = pltpu.VMEM((nc, r, t), BF16)
    field32 = pltpu.VMEM((nc, r, t), F32)
    flops = 2 * 2 * time * 3 * (g2 * 2 * r + po * g)
    args = (sig, w, wb, p, pb, ct, cs)
    outs = pl.pallas_call(
        functools.partial(kernel, cfg),
        out_shape=(
            jax.ShapeDtypeStruct(sig.shape, BF16),
            jax.ShapeDtypeStruct(sig.shape, BF16),
            jax.ShapeDtypeStruct(sig.shape, BF16),
            jax.ShapeDtypeStruct(w.shape, F32),
            jax.ShapeDtypeStruct(wb.shape, F32),
            jax.ShapeDtypeStruct(p.shape, F32),
            jax.ShapeDtypeStruct(pb.shape, F32),
        ),
        in_specs=[hbm] * 7,
        out_specs=[hbm] * 7,
        scratch_shapes=[pltpu.VMEM(a.shape, a.dtype) for a in args]
        + [
            dma((7,)),
            pltpu.VMEM(sig.shape, BF16),
            pltpu.VMEM(sig.shape, BF16),
            pltpu.VMEM(sig.shape, BF16),
            pltpu.VMEM(w.shape, F32),
            pltpu.VMEM(wb.shape, F32),
            pltpu.VMEM(p.shape, F32),
            pltpu.VMEM(pb.shape, F32),
            dma((7,)),
            field,
            field,
            field,
            field,
            field,
            field,
            field,
            pltpu.VMEM((nc, g, t), F32),
            pltpu.VMEM((nc, g, t), F32),
            pltpu.VMEM((nc, g, t), BF16),
            field32,
            field32,
            field32,
            pltpu.VMEM((2, w.shape[2], g2), BF16),
            pltpu.VMEM((2, g, po), BF16),
            pltpu.VMEM((2, g2, 128), F32),
            pltpu.VMEM((2, po, 128), F32),
            pltpu.VMEM((2, g2, w.shape[2]), F32),
            pltpu.VMEM((2, po, g), F32),
            pltpu.VMEM((2, g2 + po, 128), F32),
            pltpu.VMEM((16, 128), F32),
            pltpu.VMEM((ncor * rows, 128), BF16),
            pltpu.VMEM((ncor - 1, rows, 128), BF16),
            pltpu.VMEM((ntm, rows, 128), BF16),
            pltpu.VMEM((ncor * rows, 128), BF16),
        ]
        + [dma((nc,))] * 8
        + [dma((ncor - 1,))] * 2
        + [dma((ntm - 1,))] * 2
        + [dma((ncor - 1,))] * 2,
        compiler_params=pltpu.CompilerParams(
            collective_id=0, has_side_effects=True, vmem_limit_bytes=room
        ),
        cost_estimate=pl.CostEstimate(
            flops=flops, bytes_accessed=6 * sig.size * 2, transcendentals=2 * g2 * time
        ),
    )(*args)
    return pl.pallas_call(
        deliver,
        out_shape=tuple(jax.ShapeDtypeStruct(a.shape, a.dtype) for a in outs),
        in_specs=[hbm] * 7,
        out_specs=[hbm] * 7,
        scratch_shapes=[pltpu.VMEM(a.shape, a.dtype) for a in outs] + [dma((2, 7))],
        compiler_params=pltpu.CompilerParams(vmem_limit_bytes=room),
    )(*outs)


def solution(mesh):
    field = P("corner", None, "tm")
    return jax.shard_map(
        on_device,
        mesh=mesh,
        in_specs=(field, P(), P(), P(), P(), field, field),
        out_specs=(field, field, field, P(), P(), P(), P()),
        check_vma=False,
    )
```

```python
import functools
import math

import jax
import jax.numpy as jnp
from jax import lax
from jax.experimental import pallas as pl
from jax.experimental.pallas import tpu as pltpu
from jax.sharding import PartitionSpec as P

MESH = pl.DeviceIdType.MESH
F32 = jnp.float32
BF16 = jnp.bfloat16
CHUNK = 512
LAG_TOP = 1
LAG_LOW = 2
AHEAD = 2


def dot(a, b):
    return jnp.dot(a, b, preferred_element_type=F32)


def dot_nt(a, b):
    return lax.dot_general(a, b, (((1,), (1,)), ((), ())), preferred_element_type=F32)


def kernel(
    cfg,
    sig_h,
    w_h,
    wb_h,
    p_h,
    pb_h,
    ct_h,
    cs_h,
    xtop_h,
    skip_h,
    ginp_h,
    gconv_h,
    gcbias_h,
    gout_h,
    gobias_h,
    sig,
    w,
    wb,
    p,
    pb,
    ct,
    cs,
    in_s,
    xtop,
    skip,
    ginp,
    gconv,
    gcbias,
    gout,
    gobias,
    out_s,
    tap0,
    xmid,
    tap1,
    gdel1,
    d1,
    gdel0,
    d0,
    df0,
    dg0,
    z0,
    skip0,
    res1,
    res0,
    wt,
    pt,
    wbc,
    pbc,
    accw,
    accp,
    accb,
    bias,
    part,
    rs_buf,
    z_buf,
    total,
    sig_s,
    sig_r,
    x_s,
    x_r,
    d1_s,
    d1_r,
    d0_s,
    d0_r,
    rs_s,
    rs_r,
    z_s,
    z_r,
    ag_s,
    ag_r,
):
    ncor, ntm, nc, t, rows, scale = cfg
    r = sig.shape[1]
    g = p.shape[2]
    g2 = w.shape[1]
    po = p.shape[1]
    me = lax.axis_index("corner")
    zi = lax.axis_index("tm")

    def cols(i):
        return pl.ds(i * t if isinstance(i, int) else pl.multiple_of(i * t, t), t)

    def shift_copy(src, dst, ssem, rsem, i, distance):
        return pltpu.make_async_remote_copy(
            src_ref=src,
            dst_ref=dst.at[i],
            send_sem=ssem.at[i],
            recv_sem=rsem.at[i],
            device_id={"tm": lax.rem(zi + distance + ntm, ntm)},
            device_id_type=MESH,
        )

    def sig_copy(i):
        return shift_copy(sig.at[0, :, cols(i)], tap0, sig_s, sig_r, i, 1)

    def x_copy(i):
        return shift_copy(xmid.at[i], tap1, x_s, x_r, i, 2)

    def d1_copy(i):
        return shift_copy(gdel1.at[i], d1, d1_s, d1_r, i, -2)

    def d0_copy(i):
        return shift_copy(gdel0.at[i], d0, d0_s, d0_r, i, -1)

    moves = [
        pltpu.make_async_copy(a, b, in_s.at[k])
        for k, (a, b) in enumerate(
            ((sig_h, sig), (w_h, w), (wb_h, wb), (p_h, p), (pb_h, pb), (ct_h, ct), (cs_h, cs))
        )
    ]
    for m in moves:
        m.start()

    barrier = pltpu.get_barrier_semaphore()

    def greet_corner(j, carry):
        pl.semaphore_signal(
            barrier, inc=1, device_id={"corner": lax.rem(me + j, ncor)}, device_id_type=MESH
        )
        return carry

    def greet_tm(j, carry):
        pl.semaphore_signal(
            barrier, inc=1, device_id={"tm": lax.rem(zi + j, ntm)}, device_id_type=MESH
        )
        return carry

    lax.fori_loop(1, ncor, greet_corner, 0)
    lax.fori_loop(1, ntm, greet_tm, 0)

    for m in moves:
        m.wait()
    for l in range(2):
        wt[l] = w[l].astype(F32).T.astype(BF16)
        pt[l] = p[l].astype(F32).T.astype(BF16)
        wbc[l] = jnp.broadcast_to(wb[l : l + 1, :], (128, g2)).T
        pbc[l] = jnp.broadcast_to(pb[l : l + 1, :], (128, po)).T
    accw[...] = jnp.zeros_like(accw)
    accp[...] = jnp.zeros_like(accp)
    accb[...] = jnp.zeros_like(accb)
    part[...] = jnp.zeros_like(part)
    bias[...] = jnp.zeros_like(bias)

    @pl.when(zi < 1)
    def _():
        tap0[...] = jnp.zeros_like(tap0)

    @pl.when(zi < 2)
    def _():
        tap1[...] = jnp.zeros_like(tap1)

    @pl.when(zi >= ntm - 2)
    def _():
        d1[...] = jnp.zeros_like(d1)

    @pl.when(zi >= ntm - 1)
    def _():
        d0[...] = jnp.zeros_like(d0)

    pl.semaphore_wait(barrier, ncor - 1 + ntm - 1)

    def send_sig(i):
        @pl.when(zi < ntm - 1)
        def _():
            sig_copy(i).start()

    for i in range(AHEAD):
        send_sig(i)

    def fold(v):
        v = v.astype(F32)
        s = v[:, 0:128]
        for k in range(1, t // 128):
            s = s + v[:, k * 128 : (k + 1) * 128]
        return s

    def wide(ref, l):
        return jnp.concatenate([ref[l]] * (t // 128), axis=1)

    def gates(l, stacked):
        pre = dot(w[l], stacked) + wide(wbc, l)
        th = jnp.tanh(pre[:g])
        sg = 0.5 * jnp.tanh(0.5 * pre[g:]) + 0.5
        z = th * sg
        zb = z.astype(BF16)
        mixed = dot(p[l], zb) + wide(pbc, l)
        return sg - z * th, z - z * sg, zb, mixed

    def accumulate(l, gpre, stacked, u, zb):
        accw[l] += dot_nt(gpre, stacked)
        accp[l] += dot_nt(u, zb)
        accb[l, 0:g2] += fold(gpre)
        accb[l, g2 : g2 + po] += fold(u)

    def wait_sig(i):
        @pl.when(zi >= 1)
        def _():
            sig_copy(i).wait_recv()

    def send_x(i):
        @pl.when(zi < ntm - 2)
        def _():
            x_copy(i).start()

    def forward_low(i):
        a = sig[0, :, cols(i)]
        df, dg, zb, mixed = gates(0, jnp.concatenate([tap0[i], a], axis=0))
        xmid[i] = (a.astype(F32) + mixed[:r]).astype(BF16)
        df0[i] = df
        dg0[i] = dg
        z0[i] = zb
        skip0[i] = mixed[r:]

    def wait_x(i):
        @pl.when(zi >= 2)
        def _():
            x_copy(i).wait_recv()

    def send_d1(i):
        @pl.when(zi >= 2)
        def _():
            d1_copy(i).start()

    def wait_d1(i):
        @pl.when(zi < ntm - 2)
        def _():
            d1_copy(i).wait_recv()

    def send_d0(i):
        @pl.when(zi >= 1)
        def _():
            d0_copy(i).start()

    def top(i):
        a = xmid[i]
        stacked = jnp.concatenate([tap1[i], a], axis=0)
        df, dg, zb, mixed = gates(1, stacked)
        c = ct[0, :, cols(i)]
        u = jnp.concatenate([c, cs[0, :, cols(i)]], axis=0)
        gz = dot(pt[1], u)
        gpre = jnp.concatenate([gz * df, gz * dg], axis=0).astype(BF16)
        gin = dot(wt[1], gpre)
        gdel1[i] = gin[:r].astype(BF16)
        res1[i] = c.astype(F32) + gin[r:]
        xtop[0, :, cols(i)] = (a.astype(F32) + mixed[:r]).astype(BF16)
        skip[0, :, cols(i)] = (skip0[i] + mixed[r:]).astype(BF16)
        accumulate(1, gpre, stacked, u, zb)

    def low(i):
        gm = (res1[i] + d1[i].astype(F32)).astype(BF16)
        u = jnp.concatenate([gm, cs[0, :, cols(i)]], axis=0)
        gz = dot(pt[0], u)
        gpre = jnp.concatenate([gz * df0[i], gz * dg0[i]], axis=0).astype(BF16)
        gin = dot(wt[0], gpre)
        gdel0[i] = gin[:r].astype(BF16)
        res0[i] = gm.astype(F32) + gin[r:]
        stacked = jnp.concatenate([tap0[i], sig[0, :, cols(i)]], axis=0)
        accumulate(0, gpre, stacked, u, z0[i])

    def step(i, first, second, third):
        j, k = i - LAG_TOP, i - LAG_LOW
        if first:
            wait_sig(i)
            forward_low(i)
            send_x(i)
            if not isinstance(i, int):

                @pl.when(i + AHEAD < nc)
                def _():
                    send_sig(i + AHEAD)

            elif i + AHEAD < nc:
                send_sig(i + AHEAD)
        if second:
            wait_x(j)
            top(j)
            send_d1(j)
        if third:
            wait_d1(k)
            low(k)
            send_d0(k)

    def finish(i, carry):
        @pl.when(zi < ntm - 1)
        def _():
            d0_copy(i).wait_recv()

        ginp[0, :, cols(i)] = (res0[i] + d0[i].astype(F32)).astype(BF16)
        return carry

    def shard(k):
        return pl.ds(pl.multiple_of(k * rows, 16), rows)

    def reduce_copy(src, dst, ssem, rsem, j, axis, to):
        return pltpu.make_async_remote_copy(
            src_ref=src,
            dst_ref=dst,
            send_sem=ssem.at[j - 1],
            recv_sem=rsem.at[j - 1],
            device_id={axis: to},
            device_id_type=MESH,
        )

    def rs_copy(j):
        to = lax.rem(me + j, ncor)
        return reduce_copy(part.at[shard(to)], rs_buf.at[j - 1], rs_s, rs_r, j, "corner", to)

    def z_copy(j, slot):
        to = lax.rem(zi + j, ntm)
        return reduce_copy(z_buf.at[zi], z_buf.at[slot], z_s, z_r, j, "tm", to)

    def ag_copy(j, owner):
        to = lax.rem(me + j, ncor)
        return reduce_copy(
            total.at[shard(me)], total.at[shard(owner)], ag_s, ag_r, j, "corner", to
        )

    def z_from(j):
        return lax.rem(zi - j + ntm, ntm)

    def ag_from(j):
        return lax.rem(me - j + ncor, ncor)

    def put(src, dst, k):
        return pltpu.make_async_copy(src, dst, out_s.at[k])

    def each(n, body):
        def step(j, carry):
            body(j)
            return carry

        lax.fori_loop(1, n, step, 0)

    mats = g2 + po
    cuts = g2 // 128

    def fill(l):
        part[l * mats : l * mats + g2] = accw[l].astype(BF16)
        part[l * mats + g2 : (l + 1) * mats] = accp[l].astype(BF16)
        brow = jnp.sum(accb[l].T, axis=0, keepdims=True)
        for k in range(cuts + 1):
            at = l * (cuts + 1) + k
            bias[at : at + 1] = brow[:, k * 128 : (k + 1) * 128]

    def rs_start():
        part[2 * mats : 2 * mats + 16] = bias[...].astype(BF16)
        each(ncor, lambda j: rs_copy(j).start())

    def z_start():
        each(ncor, lambda j: rs_copy(j).wait_recv())
        s = part[shard(me)].astype(F32)
        for j in range(ncor - 1):
            s = s + rs_buf[j].astype(F32)
        z_buf[zi] = s.astype(BF16)
        each(ntm, lambda j: z_copy(j, zi).start())

    def ag_start():
        each(ntm, lambda j: z_copy(j, z_from(j)).wait_recv())
        s = z_buf[0].astype(F32)
        for j in range(1, ntm):
            s = s + z_buf[j].astype(F32)
        total[shard(me)] = (s * scale).astype(BF16)
        each(ncor, lambda j: ag_copy(j, me).start())

    def ag_finish():
        each(ncor, lambda j: ag_copy(j, ag_from(j)).wait_recv())
        tail = total[2 * mats : 2 * mats + 16].astype(F32)
        for l in range(2):
            gconv[l] = total[l * mats : l * mats + g2].astype(F32)
            gout[l] = total[l * mats + g2 : (l + 1) * mats].astype(F32)
            for k in range(cuts):
                at = l * (cuts + 1) + k
                gcbias[l : l + 1, k * 128 : (k + 1) * 128] = tail[at : at + 1]
            at = l * (cuts + 1) + cuts
            gobias[l : l + 1, :] = tail[at : at + 1]

    def full(i, carry):
        step(i, True, True, True)
        return carry

    for i in range(LAG_LOW):
        step(i, True, i >= LAG_TOP, False)
    lax.fori_loop(LAG_LOW, nc, full, 0)
    for i in range(nc, nc + LAG_TOP):
        step(i, False, True, True)
    put(xtop, xtop_h, 0).start()
    put(skip, skip_h, 1).start()
    fill(1)
    for i in range(nc + LAG_TOP, nc + LAG_LOW):
        step(i, False, False, True)
    fill(0)
    rs_start()
    z_start()
    lax.fori_loop(0, nc, finish, 0)
    put(ginp, ginp_h, 2).start()
    ag_start()
    ag_finish()
    for k, (a, b) in enumerate(
        ((gconv, gconv_h), (gcbias, gcbias_h), (gout, gout_h), (gobias, gobias_h))
    ):
        put(a, b, 3 + k).start()

    def sent(i, carry):
        @pl.when(zi < ntm - 1)
        def _():
            sig_copy(i).wait_send()

        @pl.when(zi < ntm - 2)
        def _():
            x_copy(i).wait_send()

        @pl.when(zi >= 2)
        def _():
            d1_copy(i).wait_send()

        @pl.when(zi >= 1)
        def _():
            d0_copy(i).wait_send()

        return carry

    lax.fori_loop(0, nc, sent, 0)
    each(ncor, lambda j: rs_copy(j).wait_send())
    each(ntm, lambda j: z_copy(j, zi).wait_send())
    each(ncor, lambda j: ag_copy(j, me).wait_send())
    for k, (a, b) in enumerate(
        (
            (xtop, xtop_h),
            (skip, skip_h),
            (ginp, ginp_h),
            (gconv, gconv_h),
            (gcbias, gcbias_h),
            (gout, gout_h),
            (gobias, gobias_h),
        )
    ):
        put(a, b, k).wait()


def deliver(*refs):
    held, sems = refs[14:21], refs[21]
    ins = [pltpu.make_async_copy(refs[k], held[k], sems.at[0, k]) for k in range(7)]
    outs = [pltpu.make_async_copy(held[k], refs[7 + k], sems.at[1, k]) for k in range(7)]
    for m in ins:
        m.start()
    for a, b in zip(ins, outs):
        a.wait()
        b.start()
    for b in outs:
        b.wait()


def on_device(sig, w, wb, p, pb, ct, cs):
    ncor = lax.axis_size("corner")
    ntm = lax.axis_size("tm")
    _, r, time = sig.shape
    _, g2, _ = w.shape
    _, po, g = p.shape
    t = CHUNK
    nc = time // t
    used = 2 * (g2 + po) + 16
    rows = -(-used // (ncor * 16)) * 16
    count = sig.shape[0] * ncor * time * ntm
    cfg = (ncor, ntm, nc, t, rows, 1.0 / math.sqrt(count))
    hbm = pl.BlockSpec(memory_space=pltpu.HBM)
    room = 62 * 1024 * 1024
    dma = pltpu.SemaphoreType.DMA
    field = pltpu.VMEM((nc, r, t), BF16)
    field32 = pltpu.VMEM((nc, r, t), F32)
    flops = 2 * 2 * time * 3 * (g2 * 2 * r + po * g)
    args = (sig, w, wb, p, pb, ct, cs)
    outs = pl.pallas_call(
        functools.partial(kernel, cfg),
        out_shape=(
            jax.ShapeDtypeStruct(sig.shape, BF16),
            jax.ShapeDtypeStruct(sig.shape, BF16),
            jax.ShapeDtypeStruct(sig.shape, BF16),
            jax.ShapeDtypeStruct(w.shape, F32),
            jax.ShapeDtypeStruct(wb.shape, F32),
            jax.ShapeDtypeStruct(p.shape, F32),
            jax.ShapeDtypeStruct(pb.shape, F32),
        ),
        in_specs=[hbm] * 7,
        out_specs=[hbm] * 7,
        scratch_shapes=[pltpu.VMEM(a.shape, a.dtype) for a in args]
        + [
            dma((7,)),
            pltpu.VMEM(sig.shape, BF16),
            pltpu.VMEM(sig.shape, BF16),
            pltpu.VMEM(sig.shape, BF16),
            pltpu.VMEM(w.shape, F32),
            pltpu.VMEM(wb.shape, F32),
            pltpu.VMEM(p.shape, F32),
            pltpu.VMEM(pb.shape, F32),
            dma((7,)),
            field,
            field,
            field,
            field,
            field,
            field,
            field,
            pltpu.VMEM((nc, g, t), F32),
            pltpu.VMEM((nc, g, t), F32),
            pltpu.VMEM((nc, g, t), BF16),
            field32,
            field32,
            field32,
            pltpu.VMEM((2, w.shape[2], g2), BF16),
            pltpu.VMEM((2, g, po), BF16),
            pltpu.VMEM((2, g2, 128), F32),
            pltpu.VMEM((2, po, 128), F32),
            pltpu.VMEM((2, g2, w.shape[2]), F32),
            pltpu.VMEM((2, po, g), F32),
            pltpu.VMEM((2, g2 + po, 128), F32),
            pltpu.VMEM((16, 128), F32),
            pltpu.VMEM((ncor * rows, 128), BF16),
            pltpu.VMEM((ncor - 1, rows, 128), BF16),
            pltpu.VMEM((ntm, rows, 128), BF16),
            pltpu.VMEM((ncor * rows, 128), BF16),
        ]
        + [dma((nc,))] * 8
        + [dma((ncor - 1,))] * 2
        + [dma((ntm - 1,))] * 2
        + [dma((ncor - 1,))] * 2,
        compiler_params=pltpu.CompilerParams(
            collective_id=0, has_side_effects=True, vmem_limit_bytes=room
        ),
        cost_estimate=pl.CostEstimate(
            flops=flops, bytes_accessed=6 * sig.size * 2, transcendentals=2 * g2 * time
        ),
    )(*args)
    return pl.pallas_call(
        deliver,
        out_shape=tuple(jax.ShapeDtypeStruct(a.shape, a.dtype) for a in outs),
        in_specs=[hbm] * 7,
        out_specs=[hbm] * 7,
        scratch_shapes=[pltpu.VMEM(a.shape, a.dtype) for a in outs] + [dma((2, 7))],
        compiler_params=pltpu.CompilerParams(vmem_limit_bytes=room),
    )(*outs)


def solution(mesh):
    field = P("corner", None, "tm")
    return jax.shard_map(
        on_device,
        mesh=mesh,
        in_specs=(field, P(), P(), P(), P(), field, field),
        out_specs=(field, field, field, P(), P(), P(), P()),
        check_vma=False,
    )
```

```python
import functools
import math

import jax
import jax.numpy as jnp
from jax import lax
from jax.experimental import pallas as pl
from jax.experimental.pallas import tpu as pltpu
from jax.sharding import PartitionSpec as P

MESH = pl.DeviceIdType.MESH
F32 = jnp.float32
BF16 = jnp.bfloat16
CHUNK = 256
LAG_TOP = 2
LAG_LOW = 6
AHEAD = 3


def dot(a, b):
    return jnp.dot(a, b, preferred_element_type=F32)


def dot_nt(a, b):
    return lax.dot_general(a, b, (((1,), (1,)), ((), ())), preferred_element_type=F32)


def kernel(
    cfg,
    sig_h,
    w_h,
    wb_h,
    p_h,
    pb_h,
    ct_h,
    cs_h,
    xtop_h,
    skip_h,
    ginp_h,
    gconv_h,
    gcbias_h,
    gout_h,
    gobias_h,
    sig,
    w,
    wb,
    p,
    pb,
    ct,
    cs,
    in_s,
    xtop,
    skip,
    ginp,
    gconv,
    gcbias,
    gout,
    gobias,
    out_s,
    tap0,
    xmid,
    tap1,
    gdel1,
    d1,
    gdel0,
    d0,
    df0,
    dg0,
    z0,
    skip0,
    res1,
    res0,
    wt,
    pt,
    wbc,
    pbc,
    accw,
    accp,
    accb,
    bias,
    part,
    rs_buf,
    z_buf,
    total,
    sig_s,
    sig_r,
    x_s,
    x_r,
    d1_s,
    d1_r,
    d0_s,
    d0_r,
    rs_s,
    rs_r,
    z_s,
    z_r,
    ag_s,
    ag_r,
):
    ncor, ntm, nc, t, rows, scale = cfg
    r = sig.shape[1]
    g = p.shape[2]
    g2 = w.shape[1]
    po = p.shape[1]
    me = lax.axis_index("corner")
    zi = lax.axis_index("tm")

    def cols(i):
        return pl.ds(i * t if isinstance(i, int) else pl.multiple_of(i * t, t), t)

    def shift_copy(src, dst, ssem, rsem, i, distance):
        return pltpu.make_async_remote_copy(
            src_ref=src,
            dst_ref=dst.at[i],
            send_sem=ssem.at[i],
            recv_sem=rsem.at[i],
            device_id={"tm": lax.rem(zi + distance + ntm, ntm)},
            device_id_type=MESH,
        )

    def sig_copy(i):
        return shift_copy(sig.at[0, :, cols(i)], tap0, sig_s, sig_r, i, 1)

    def x_copy(i):
        return shift_copy(xmid.at[i], tap1, x_s, x_r, i, 2)

    def d1_copy(i):
        return shift_copy(gdel1.at[i], d1, d1_s, d1_r, i, -2)

    def d0_copy(i):
        return shift_copy(gdel0.at[i], d0, d0_s, d0_r, i, -1)

    moves = [
        pltpu.make_async_copy(a, b, in_s.at[k])
        for k, (a, b) in enumerate(
            ((sig_h, sig), (w_h, w), (wb_h, wb), (p_h, p), (pb_h, pb), (ct_h, ct), (cs_h, cs))
        )
    ]
    for m in moves:
        m.start()

    barrier = pltpu.get_barrier_semaphore()

    def greet_corner(j, carry):
        pl.semaphore_signal(
            barrier, inc=1, device_id={"corner": lax.rem(me + j, ncor)}, device_id_type=MESH
        )
        return carry

    def greet_tm(j, carry):
        pl.semaphore_signal(
            barrier, inc=1, device_id={"tm": lax.rem(zi + j, ntm)}, device_id_type=MESH
        )
        return carry

    lax.fori_loop(1, ncor, greet_corner, 0)
    lax.fori_loop(1, ntm, greet_tm, 0)

    for m in moves:
        m.wait()
    for l in range(2):
        wt[l] = w[l].astype(F32).T.astype(BF16)
        pt[l] = p[l].astype(F32).T.astype(BF16)
        wbc[l] = jnp.broadcast_to(wb[l : l + 1, :], (128, g2)).T
        pbc[l] = jnp.broadcast_to(pb[l : l + 1, :], (128, po)).T
    accw[...] = jnp.zeros_like(accw)
    accp[...] = jnp.zeros_like(accp)
    accb[...] = jnp.zeros_like(accb)
    part[...] = jnp.zeros_like(part)
    bias[...] = jnp.zeros_like(bias)

    @pl.when(zi < 1)
    def _():
        tap0[...] = jnp.zeros_like(tap0)

    @pl.when(zi < 2)
    def _():
        tap1[...] = jnp.zeros_like(tap1)

    @pl.when(zi >= ntm - 2)
    def _():
        d1[...] = jnp.zeros_like(d1)

    @pl.when(zi >= ntm - 1)
    def _():
        d0[...] = jnp.zeros_like(d0)

    pl.semaphore_wait(barrier, ncor - 1 + ntm - 1)

    def send_sig(i):
        @pl.when(zi < ntm - 1)
        def _():
            sig_copy(i).start()

    for i in range(AHEAD):
        send_sig(i)

    def fold(v):
        v = v.astype(F32)
        s = v[:, 0:128]
        for k in range(1, t // 128):
            s = s + v[:, k * 128 : (k + 1) * 128]
        return s

    def wide(ref, l):
        return jnp.concatenate([ref[l]] * (t // 128), axis=1)

    def gates(l, stacked):
        pre = dot(w[l], stacked) + wide(wbc, l)
        th = jnp.tanh(pre[:g])
        sg = 0.5 * jnp.tanh(0.5 * pre[g:]) + 0.5
        z = th * sg
        zb = z.astype(BF16)
        mixed = dot(p[l], zb) + wide(pbc, l)
        return sg - z * th, z - z * sg, zb, mixed

    def accumulate(l, gpre, stacked, u, zb):
        accw[l] += dot_nt(gpre, stacked)
        accp[l] += dot_nt(u, zb)
        accb[l, 0:g2] += fold(gpre)
        accb[l, g2 : g2 + po] += fold(u)

    def wait_sig(i):
        @pl.when(zi >= 1)
        def _():
            sig_copy(i).wait_recv()

    def send_x(i):
        @pl.when(zi < ntm - 2)
        def _():
            x_copy(i).start()

    def forward_low(i):
        a = sig[0, :, cols(i)]
        df, dg, zb, mixed = gates(0, jnp.concatenate([tap0[i], a], axis=0))
        xmid[i] = (a.astype(F32) + mixed[:r]).astype(BF16)
        df0[i] = df
        dg0[i] = dg
        z0[i] = zb
        skip0[i] = mixed[r:]

    def wait_x(i):
        @pl.when(zi >= 2)
        def _():
            x_copy(i).wait_recv()

    def send_d1(i):
        @pl.when(zi >= 2)
        def _():
            d1_copy(i).start()

    def wait_d1(i):
        @pl.when(zi < ntm - 2)
        def _():
            d1_copy(i).wait_recv()

    def send_d0(i):
        @pl.when(zi >= 1)
        def _():
            d0_copy(i).start()

    def top(i):
        a = xmid[i]
        stacked = jnp.concatenate([tap1[i], a], axis=0)
        df, dg, zb, mixed = gates(1, stacked)
        c = ct[0, :, cols(i)]
        u = jnp.concatenate([c, cs[0, :, cols(i)]], axis=0)
        gz = dot(pt[1], u)
        gpre = jnp.concatenate([gz * df, gz * dg], axis=0).astype(BF16)
        gin = dot(wt[1], gpre)
        gdel1[i] = gin[:r].astype(BF16)
        res1[i] = c.astype(F32) + gin[r:]
        xtop[0, :, cols(i)] = (a.astype(F32) + mixed[:r]).astype(BF16)
        skip[0, :, cols(i)] = (skip0[i] + mixed[r:]).astype(BF16)
        accumulate(1, gpre, stacked, u, zb)

    def low(i):
        gm = (res1[i] + d1[i].astype(F32)).astype(BF16)
        u = jnp.concatenate([gm, cs[0, :, cols(i)]], axis=0)
        gz = dot(pt[0], u)
        gpre = jnp.concatenate([gz * df0[i], gz * dg0[i]], axis=0).astype(BF16)
        gin = dot(wt[0], gpre)
        gdel0[i] = gin[:r].astype(BF16)
        res0[i] = gm.astype(F32) + gin[r:]
        stacked = jnp.concatenate([tap0[i], sig[0, :, cols(i)]], axis=0)
        accumulate(0, gpre, stacked, u, z0[i])

    def step(i, first, second, third):
        j, k = i - LAG_TOP, i - LAG_LOW
        if first:
            wait_sig(i)
            forward_low(i)
            send_x(i)
            if not isinstance(i, int):

                @pl.when(i + AHEAD < nc)
                def _():
                    send_sig(i + AHEAD)

            elif i + AHEAD < nc:
                send_sig(i + AHEAD)
        if second:
            wait_x(j)
            top(j)
            send_d1(j)
        if third:
            wait_d1(k)
            low(k)
            send_d0(k)

    def finish(i, carry):
        @pl.when(zi < ntm - 1)
        def _():
            d0_copy(i).wait_recv()

        ginp[0, :, cols(i)] = (res0[i] + d0[i].astype(F32)).astype(BF16)
        return carry

    def shard(k):
        return pl.ds(pl.multiple_of(k * rows, 16), rows)

    def reduce_copy(src, dst, ssem, rsem, j, axis, to):
        return pltpu.make_async_remote_copy(
            src_ref=src,
            dst_ref=dst,
            send_sem=ssem.at[j - 1],
            recv_sem=rsem.at[j - 1],
            device_id={axis: to},
            device_id_type=MESH,
        )

    def rs_copy(j):
        to = lax.rem(me + j, ncor)
        return reduce_copy(part.at[shard(to)], rs_buf.at[j - 1], rs_s, rs_r, j, "corner", to)

    def z_copy(j, slot):
        to = lax.rem(zi + j, ntm)
        return reduce_copy(z_buf.at[zi], z_buf.at[slot], z_s, z_r, j, "tm", to)

    def ag_copy(j, owner):
        to = lax.rem(me + j, ncor)
        return reduce_copy(
            total.at[shard(me)], total.at[shard(owner)], ag_s, ag_r, j, "corner", to
        )

    def z_from(j):
        return lax.rem(zi - j + ntm, ntm)

    def ag_from(j):
        return lax.rem(me - j + ncor, ncor)

    def put(src, dst, k):
        return pltpu.make_async_copy(src, dst, out_s.at[k])

    def each(n, body):
        def step(j, carry):
            body(j)
            return carry

        lax.fori_loop(1, n, step, 0)

    mats = g2 + po
    cuts = g2 // 128

    def fill(l):
        part[l * mats : l * mats + g2] = accw[l].astype(BF16)
        part[l * mats + g2 : (l + 1) * mats] = accp[l].astype(BF16)
        brow = jnp.sum(accb[l].T, axis=0, keepdims=True)
        for k in range(cuts + 1):
            at = l * (cuts + 1) + k
            bias[at : at + 1] = brow[:, k * 128 : (k + 1) * 128]

    def rs_start():
        part[2 * mats : 2 * mats + 16] = bias[...].astype(BF16)
        each(ncor, lambda j: rs_copy(j).start())

    def z_start():
        each(ncor, lambda j: rs_copy(j).wait_recv())
        s = part[shard(me)].astype(F32)
        for j in range(ncor - 1):
            s = s + rs_buf[j].astype(F32)
        z_buf[zi] = s.astype(BF16)
        each(ntm, lambda j: z_copy(j, zi).start())

    def ag_start():
        each(ntm, lambda j: z_copy(j, z_from(j)).wait_recv())
        s = z_buf[0].astype(F32)
        for j in range(1, ntm):
            s = s + z_buf[j].astype(F32)
        total[shard(me)] = (s * scale).astype(BF16)
        each(ncor, lambda j: ag_copy(j, me).start())

    def ag_finish():
        each(ncor, lambda j: ag_copy(j, ag_from(j)).wait_recv())
        tail = total[2 * mats : 2 * mats + 16].astype(F32)
        for l in range(2):
            gconv[l] = total[l * mats : l * mats + g2].astype(F32)
            gout[l] = total[l * mats + g2 : (l + 1) * mats].astype(F32)
            for k in range(cuts):
                at = l * (cuts + 1) + k
                gcbias[l : l + 1, k * 128 : (k + 1) * 128] = tail[at : at + 1]
            at = l * (cuts + 1) + cuts
            gobias[l : l + 1, :] = tail[at : at + 1]

    def steps(lo, hi, first, second, third):
        def body(i, carry):
            step(i, first, second, third)
            return carry

        lax.fori_loop(lo, hi, body, 0)

    steps(0, LAG_TOP, True, False, False)
    steps(LAG_TOP, LAG_LOW, True, True, False)
    steps(LAG_LOW, nc, True, True, True)
    steps(nc, nc + LAG_TOP, False, True, True)
    put(xtop, xtop_h, 0).start()
    put(skip, skip_h, 1).start()
    fill(1)
    steps(nc + LAG_TOP, nc + LAG_LOW, False, False, True)
    fill(0)
    rs_start()
    z_start()
    lax.fori_loop(0, nc, finish, 0)
    put(ginp, ginp_h, 2).start()
    ag_start()
    ag_finish()
    for k, (a, b) in enumerate(
        ((gconv, gconv_h), (gcbias, gcbias_h), (gout, gout_h), (gobias, gobias_h))
    ):
        put(a, b, 3 + k).start()

    def sent(i, carry):
        @pl.when(zi < ntm - 1)
        def _():
            sig_copy(i).wait_send()

        @pl.when(zi < ntm - 2)
        def _():
            x_copy(i).wait_send()

        @pl.when(zi >= 2)
        def _():
            d1_copy(i).wait_send()

        @pl.when(zi >= 1)
        def _():
            d0_copy(i).wait_send()

        return carry

    lax.fori_loop(0, nc, sent, 0)
    each(ncor, lambda j: rs_copy(j).wait_send())
    each(ntm, lambda j: z_copy(j, zi).wait_send())
    each(ncor, lambda j: ag_copy(j, me).wait_send())
    for k, (a, b) in enumerate(
        (
            (xtop, xtop_h),
            (skip, skip_h),
            (ginp, ginp_h),
            (gconv, gconv_h),
            (gcbias, gcbias_h),
            (gout, gout_h),
            (gobias, gobias_h),
        )
    ):
        put(a, b, k).wait()


def deliver(*refs):
    held, sems = refs[14:21], refs[21]
    ins = [pltpu.make_async_copy(refs[k], held[k], sems.at[0, k]) for k in range(7)]
    outs = [pltpu.make_async_copy(held[k], refs[7 + k], sems.at[1, k]) for k in range(7)]
    for m in ins:
        m.start()
    for a, b in zip(ins, outs):
        a.wait()
        b.start()
    for b in outs:
        b.wait()


def on_device(sig, w, wb, p, pb, ct, cs):
    ncor = lax.axis_size("corner")
    ntm = lax.axis_size("tm")
    _, r, time = sig.shape
    _, g2, _ = w.shape
    _, po, g = p.shape
    t = CHUNK
    nc = time // t
    used = 2 * (g2 + po) + 16
    rows = -(-used // (ncor * 16)) * 16
    count = sig.shape[0] * ncor * time * ntm
    cfg = (ncor, ntm, nc, t, rows, 1.0 / math.sqrt(count))
    hbm = pl.BlockSpec(memory_space=pltpu.HBM)
    room = 62 * 1024 * 1024
    dma = pltpu.SemaphoreType.DMA
    field = pltpu.VMEM((nc, r, t), BF16)
    field32 = pltpu.VMEM((nc, r, t), F32)
    flops = 2 * 2 * time * 3 * (g2 * 2 * r + po * g)
    args = (sig, w, wb, p, pb, ct, cs)
    outs = pl.pallas_call(
        functools.partial(kernel, cfg),
        out_shape=(
            jax.ShapeDtypeStruct(sig.shape, BF16),
            jax.ShapeDtypeStruct(sig.shape, BF16),
            jax.ShapeDtypeStruct(sig.shape, BF16),
            jax.ShapeDtypeStruct(w.shape, F32),
            jax.ShapeDtypeStruct(wb.shape, F32),
            jax.ShapeDtypeStruct(p.shape, F32),
            jax.ShapeDtypeStruct(pb.shape, F32),
        ),
        in_specs=[hbm] * 7,
        out_specs=[hbm] * 7,
        scratch_shapes=[pltpu.VMEM(a.shape, a.dtype) for a in args]
        + [
            dma((7,)),
            pltpu.VMEM(sig.shape, BF16),
            pltpu.VMEM(sig.shape, BF16),
            pltpu.VMEM(sig.shape, BF16),
            pltpu.VMEM(w.shape, F32),
            pltpu.VMEM(wb.shape, F32),
            pltpu.VMEM(p.shape, F32),
            pltpu.VMEM(pb.shape, F32),
            dma((7,)),
            field,
            field,
            field,
            field,
            field,
            field,
            field,
            pltpu.VMEM((nc, g, t), F32),
            pltpu.VMEM((nc, g, t), F32),
            pltpu.VMEM((nc, g, t), BF16),
            field32,
            field32,
            field32,
            pltpu.VMEM((2, w.shape[2], g2), BF16),
            pltpu.VMEM((2, g, po), BF16),
            pltpu.VMEM((2, g2, 128), F32),
            pltpu.VMEM((2, po, 128), F32),
            pltpu.VMEM((2, g2, w.shape[2]), F32),
            pltpu.VMEM((2, po, g), F32),
            pltpu.VMEM((2, g2 + po, 128), F32),
            pltpu.VMEM((16, 128), F32),
            pltpu.VMEM((ncor * rows, 128), BF16),
            pltpu.VMEM((ncor - 1, rows, 128), BF16),
            pltpu.VMEM((ntm, rows, 128), BF16),
            pltpu.VMEM((ncor * rows, 128), BF16),
        ]
        + [dma((nc,))] * 8
        + [dma((ncor - 1,))] * 2
        + [dma((ntm - 1,))] * 2
        + [dma((ncor - 1,))] * 2,
        compiler_params=pltpu.CompilerParams(
            collective_id=0, has_side_effects=True, vmem_limit_bytes=room
        ),
        cost_estimate=pl.CostEstimate(
            flops=flops, bytes_accessed=6 * sig.size * 2, transcendentals=2 * g2 * time
        ),
    )(*args)
    return pl.pallas_call(
        deliver,
        out_shape=tuple(jax.ShapeDtypeStruct(a.shape, a.dtype) for a in outs),
        in_specs=[hbm] * 7,
        out_specs=[hbm] * 7,
        scratch_shapes=[pltpu.VMEM(a.shape, a.dtype) for a in outs] + [dma((2, 7))],
        compiler_params=pltpu.CompilerParams(vmem_limit_bytes=room),
    )(*outs)


def solution(mesh):
    field = P("corner", None, "tm")
    return jax.shard_map(
        on_device,
        mesh=mesh,
        in_specs=(field, P(), P(), P(), P(), field, field),
        out_specs=(field, field, field, P(), P(), P(), P()),
        check_vma=False,
    )
```

```python
import functools
import math

import jax
import jax.numpy as jnp
from jax import lax
from jax.experimental import pallas as pl
from jax.experimental.pallas import tpu as pltpu
from jax.sharding import PartitionSpec as P

MESH = pl.DeviceIdType.MESH
F32 = jnp.float32
BF16 = jnp.bfloat16
CHUNK = 512
LAG_TOP = 1
LAG_LOW = 3
AHEAD = 2


def dot(a, b):
    return jnp.dot(a, b, preferred_element_type=F32)


def dot_nt(a, b):
    return lax.dot_general(a, b, (((1,), (1,)), ((), ())), preferred_element_type=F32)


def kernel(
    cfg,
    sig_h,
    w_h,
    wb_h,
    p_h,
    pb_h,
    ct_h,
    cs_h,
    xtop_h,
    skip_h,
    ginp_h,
    gconv_h,
    gcbias_h,
    gout_h,
    gobias_h,
    sig,
    w,
    wb,
    p,
    pb,
    ct,
    cs,
    in_s,
    xtop,
    skip,
    ginp,
    gconv,
    gcbias,
    gout,
    gobias,
    out_s,
    tap0,
    xmid,
    tap1,
    gdel1,
    d1,
    gdel0,
    d0,
    df0,
    dg0,
    z0,
    skip0,
    res1,
    res0,
    wt,
    pt,
    wbc,
    pbc,
    accw,
    accp,
    accb,
    bias,
    part,
    rs_buf,
    z_buf,
    total,
    sig_s,
    sig_r,
    x_s,
    x_r,
    d1_s,
    d1_r,
    d0_s,
    d0_r,
    rs_s,
    rs_r,
    z_s,
    z_r,
    ag_s,
    ag_r,
):
    ncor, ntm, nc, t, rows, scale = cfg
    r = sig.shape[1]
    g = p.shape[2]
    g2 = w.shape[1]
    po = p.shape[1]
    me = lax.axis_index("corner")
    zi = lax.axis_index("tm")

    def cols(i):
        return pl.ds(i * t if isinstance(i, int) else pl.multiple_of(i * t, t), t)

    def shift_copy(src, dst, ssem, rsem, i, distance):
        return pltpu.make_async_remote_copy(
            src_ref=src,
            dst_ref=dst.at[i],
            send_sem=ssem.at[i],
            recv_sem=rsem.at[i],
            device_id={"tm": lax.rem(zi + distance + ntm, ntm)},
            device_id_type=MESH,
        )

    def sig_copy(i):
        return shift_copy(sig.at[0, :, cols(i)], tap0, sig_s, sig_r, i, 1)

    def x_copy(i):
        return shift_copy(xmid.at[i], tap1, x_s, x_r, i, 2)

    def d1_copy(i):
        return shift_copy(gdel1.at[i], d1, d1_s, d1_r, i, -2)

    def d0_copy(i):
        return shift_copy(gdel0.at[i], d0, d0_s, d0_r, i, -1)

    moves = [
        pltpu.make_async_copy(a, b, in_s.at[k])
        for k, (a, b) in enumerate(
            ((sig_h, sig), (w_h, w), (wb_h, wb), (p_h, p), (pb_h, pb), (ct_h, ct), (cs_h, cs))
        )
    ]
    for m in moves:
        m.start()

    barrier = pltpu.get_barrier_semaphore()

    def greet_corner(j, carry):
        pl.semaphore_signal(
            barrier, inc=1, device_id={"corner": lax.rem(me + j, ncor)}, device_id_type=MESH
        )
        return carry

    def greet_tm(j, carry):
        pl.semaphore_signal(
            barrier, inc=1, device_id={"tm": lax.rem(zi + j, ntm)}, device_id_type=MESH
        )
        return carry

    lax.fori_loop(1, ncor, greet_corner, 0)
    lax.fori_loop(1, ntm, greet_tm, 0)

    for m in moves:
        m.wait()
    for l in range(2):
        wt[l] = w[l].astype(F32).T.astype(BF16)
        pt[l] = p[l].astype(F32).T.astype(BF16)
        wbc[l] = jnp.broadcast_to(wb[l : l + 1, :], (128, g2)).T
        pbc[l] = jnp.broadcast_to(pb[l : l + 1, :], (128, po)).T
    accw[...] = jnp.zeros_like(accw)
    accp[...] = jnp.zeros_like(accp)
    accb[...] = jnp.zeros_like(accb)
    part[...] = jnp.zeros_like(part)
    bias[...] = jnp.zeros_like(bias)

    @pl.when(zi < 1)
    def _():
        tap0[...] = jnp.zeros_like(tap0)

    @pl.when(zi < 2)
    def _():
        tap1[...] = jnp.zeros_like(tap1)

    @pl.when(zi >= ntm - 2)
    def _():
        d1[...] = jnp.zeros_like(d1)

    @pl.when(zi >= ntm - 1)
    def _():
        d0[...] = jnp.zeros_like(d0)

    pl.semaphore_wait(barrier, ncor - 1 + ntm - 1)

    def send_sig(i):
        @pl.when(zi < ntm - 1)
        def _():
            sig_copy(i).start()

    for i in range(AHEAD):
        send_sig(i)

    def fold(v):
        v = v.astype(F32)
        s = v[:, 0:128]
        for k in range(1, t // 128):
            s = s + v[:, k * 128 : (k + 1) * 128]
        return s

    def wide(ref, l):
        return jnp.concatenate([ref[l]] * (t // 128), axis=1)

    def gates(l, stacked):
        pre = dot(w[l], stacked) + wide(wbc, l)
        th = jnp.tanh(pre[:g])
        sg = 0.5 * jnp.tanh(0.5 * pre[g:]) + 0.5
        z = th * sg
        zb = z.astype(BF16)
        mixed = dot(p[l], zb) + wide(pbc, l)
        return sg - z * th, z - z * sg, zb, mixed

    def accumulate(l, gpre, stacked, u, zb):
        accw[l] += dot_nt(gpre, stacked)
        accp[l] += dot_nt(u, zb)
        accb[l, 0:g2] += fold(gpre)
        accb[l, g2 : g2 + po] += fold(u)

    def wait_sig(i):
        @pl.when(zi >= 1)
        def _():
            sig_copy(i).wait_recv()

    def send_x(i):
        @pl.when(zi < ntm - 2)
        def _():
            x_copy(i).start()

    def forward_low(i):
        a = sig[0, :, cols(i)]
        df, dg, zb, mixed = gates(0, jnp.concatenate([tap0[i], a], axis=0))
        xmid[i] = (a.astype(F32) + mixed[:r]).astype(BF16)
        df0[i] = df
        dg0[i] = dg
        z0[i] = zb
        skip0[i] = mixed[r:]

    def wait_x(i):
        @pl.when(zi >= 2)
        def _():
            x_copy(i).wait_recv()

    def send_d1(i):
        @pl.when(zi >= 2)
        def _():
            d1_copy(i).start()

    def wait_d1(i):
        @pl.when(zi < ntm - 2)
        def _():
            d1_copy(i).wait_recv()

    def send_d0(i):
        @pl.when(zi >= 1)
        def _():
            d0_copy(i).start()

    def top(i):
        a = xmid[i]
        stacked = jnp.concatenate([tap1[i], a], axis=0)
        df, dg, zb, mixed = gates(1, stacked)
        c = ct[0, :, cols(i)]
        u = jnp.concatenate([c, cs[0, :, cols(i)]], axis=0)
        gz = dot(pt[1], u)
        gpre = jnp.concatenate([gz * df, gz * dg], axis=0).astype(BF16)
        gin = dot(wt[1], gpre)
        gdel1[i] = gin[:r].astype(BF16)
        res1[i] = c.astype(F32) + gin[r:]
        xtop[0, :, cols(i)] = (a.astype(F32) + mixed[:r]).astype(BF16)
        skip[0, :, cols(i)] = (skip0[i] + mixed[r:]).astype(BF16)
        accumulate(1, gpre, stacked, u, zb)

    def low(i):
        gm = (res1[i] + d1[i].astype(F32)).astype(BF16)
        u = jnp.concatenate([gm, cs[0, :, cols(i)]], axis=0)
        gz = dot(pt[0], u)
        gpre = jnp.concatenate([gz * df0[i], gz * dg0[i]], axis=0).astype(BF16)
        gin = dot(wt[0], gpre)
        gdel0[i] = gin[:r].astype(BF16)
        res0[i] = gm.astype(F32) + gin[r:]
        stacked = jnp.concatenate([tap0[i], sig[0, :, cols(i)]], axis=0)
        accumulate(0, gpre, stacked, u, z0[i])

    def step(i, first, second, third):
        j, k = i - LAG_TOP, i - LAG_LOW
        if first:
            wait_sig(i)
            forward_low(i)
            send_x(i)
            if not isinstance(i, int):

                @pl.when(i + AHEAD < nc)
                def _():
                    send_sig(i + AHEAD)

            elif i + AHEAD < nc:
                send_sig(i + AHEAD)
        if second:
            wait_x(j)
            top(j)
            send_d1(j)
        if third:
            wait_d1(k)
            low(k)
            send_d0(k)

    def finish(i, carry):
        @pl.when(zi < ntm - 1)
        def _():
            d0_copy(i).wait_recv()

        ginp[0, :, cols(i)] = (res0[i] + d0[i].astype(F32)).astype(BF16)
        return carry

    def shard(k):
        return pl.ds(pl.multiple_of(k * rows, 16), rows)

    def reduce_copy(src, dst, ssem, rsem, j, axis, to):
        return pltpu.make_async_remote_copy(
            src_ref=src,
            dst_ref=dst,
            send_sem=ssem.at[j - 1],
            recv_sem=rsem.at[j - 1],
            device_id={axis: to},
            device_id_type=MESH,
        )

    def rs_copy(j):
        to = lax.rem(me + j, ncor)
        return reduce_copy(part.at[shard(to)], rs_buf.at[j - 1], rs_s, rs_r, j, "corner", to)

    def z_copy(j, slot):
        to = lax.rem(zi + j, ntm)
        return reduce_copy(z_buf.at[zi], z_buf.at[slot], z_s, z_r, j, "tm", to)

    def ag_copy(j, owner):
        to = lax.rem(me + j, ncor)
        return reduce_copy(
            total.at[shard(me)], total.at[shard(owner)], ag_s, ag_r, j, "corner", to
        )

    def z_from(j):
        return lax.rem(zi - j + ntm, ntm)

    def ag_from(j):
        return lax.rem(me - j + ncor, ncor)

    def put(src, dst, k):
        return pltpu.make_async_copy(src, dst, out_s.at[k])

    def each(n, body):
        def step(j, carry):
            body(j)
            return carry

        lax.fori_loop(1, n, step, 0)

    mats = g2 + po
    cuts = g2 // 128

    def fill(l):
        part[l * mats : l * mats + g2] = accw[l].astype(BF16)
        part[l * mats + g2 : (l + 1) * mats] = accp[l].astype(BF16)
        brow = jnp.sum(accb[l].T, axis=0, keepdims=True)
        for k in range(cuts + 1):
            at = l * (cuts + 1) + k
            bias[at : at + 1] = brow[:, k * 128 : (k + 1) * 128]

    def rs_start():
        part[2 * mats : 2 * mats + 16] = bias[...].astype(BF16)
        each(ncor, lambda j: rs_copy(j).start())

    def z_start():
        each(ncor, lambda j: rs_copy(j).wait_recv())
        s = part[shard(me)].astype(F32)
        for j in range(ncor - 1):
            s = s + rs_buf[j].astype(F32)
        z_buf[zi] = s.astype(BF16)
        each(ntm, lambda j: z_copy(j, zi).start())

    def ag_start():
        each(ntm, lambda j: z_copy(j, z_from(j)).wait_recv())
        s = z_buf[0].astype(F32)
        for j in range(1, ntm):
            s = s + z_buf[j].astype(F32)
        total[shard(me)] = (s * scale).astype(BF16)
        each(ncor, lambda j: ag_copy(j, me).start())

    def ag_finish():
        each(ncor, lambda j: ag_copy(j, ag_from(j)).wait_recv())
        tail = total[2 * mats : 2 * mats + 16].astype(F32)
        for l in range(2):
            gconv[l] = total[l * mats : l * mats + g2].astype(F32)
            gout[l] = total[l * mats + g2 : (l + 1) * mats].astype(F32)
            for k in range(cuts):
                at = l * (cuts + 1) + k
                gcbias[l : l + 1, k * 128 : (k + 1) * 128] = tail[at : at + 1]
            at = l * (cuts + 1) + cuts
            gobias[l : l + 1, :] = tail[at : at + 1]

    def full(i, carry):
        step(i, True, True, True)
        return carry

    for i in range(LAG_LOW):
        step(i, True, i >= LAG_TOP, False)
    lax.fori_loop(LAG_LOW, nc, full, 0)
    for i in range(nc, nc + LAG_TOP):
        step(i, False, True, True)
    put(xtop, xtop_h, 0).start()
    put(skip, skip_h, 1).start()
    fill(1)
    for i in range(nc + LAG_TOP, nc + LAG_LOW):
        step(i, False, False, True)
    fill(0)
    rs_start()
    z_start()
    lax.fori_loop(0, nc, finish, 0)
    put(ginp, ginp_h, 2).start()
    ag_start()
    ag_finish()
    for k, (a, b) in enumerate(
        ((gconv, gconv_h), (gcbias, gcbias_h), (gout, gout_h), (gobias, gobias_h))
    ):
        put(a, b, 3 + k).start()

    def sent(i, carry):
        @pl.when(zi < ntm - 1)
        def _():
            sig_copy(i).wait_send()

        @pl.when(zi < ntm - 2)
        def _():
            x_copy(i).wait_send()

        @pl.when(zi >= 2)
        def _():
            d1_copy(i).wait_send()

        @pl.when(zi >= 1)
        def _():
            d0_copy(i).wait_send()

        return carry

    lax.fori_loop(0, nc, sent, 0)
    each(ncor, lambda j: rs_copy(j).wait_send())
    each(ntm, lambda j: z_copy(j, zi).wait_send())
    each(ncor, lambda j: ag_copy(j, me).wait_send())
    for k, (a, b) in enumerate(
        (
            (xtop, xtop_h),
            (skip, skip_h),
            (ginp, ginp_h),
            (gconv, gconv_h),
            (gcbias, gcbias_h),
            (gout, gout_h),
            (gobias, gobias_h),
        )
    ):
        put(a, b, k).wait()


def deliver(*refs):
    held, sems = refs[14:21], refs[21]
    ins = [pltpu.make_async_copy(refs[k], held[k], sems.at[0, k]) for k in range(7)]
    outs = [pltpu.make_async_copy(held[k], refs[7 + k], sems.at[1, k]) for k in range(7)]
    for m in ins:
        m.start()
    for a, b in zip(ins, outs):
        a.wait()
        b.start()
    for b in outs:
        b.wait()


def on_device(sig, w, wb, p, pb, ct, cs):
    ncor = lax.axis_size("corner")
    ntm = lax.axis_size("tm")
    _, r, time = sig.shape
    _, g2, _ = w.shape
    _, po, g = p.shape
    t = CHUNK
    nc = time // t
    used = 2 * (g2 + po) + 16
    rows = -(-used // (ncor * 16)) * 16
    count = sig.shape[0] * ncor * time * ntm
    cfg = (ncor, ntm, nc, t, rows, 1.0 / math.sqrt(count))
    hbm = pl.BlockSpec(memory_space=pltpu.HBM)
    room = 62 * 1024 * 1024
    dma = pltpu.SemaphoreType.DMA
    field = pltpu.VMEM((nc, r, t), BF16)
    field32 = pltpu.VMEM((nc, r, t), F32)
    flops = 2 * 2 * time * 3 * (g2 * 2 * r + po * g)
    args = (sig, w, wb, p, pb, ct, cs)
    outs = pl.pallas_call(
        functools.partial(kernel, cfg),
        out_shape=(
            jax.ShapeDtypeStruct(sig.shape, BF16),
            jax.ShapeDtypeStruct(sig.shape, BF16),
            jax.ShapeDtypeStruct(sig.shape, BF16),
            jax.ShapeDtypeStruct(w.shape, F32),
            jax.ShapeDtypeStruct(wb.shape, F32),
            jax.ShapeDtypeStruct(p.shape, F32),
            jax.ShapeDtypeStruct(pb.shape, F32),
        ),
        in_specs=[hbm] * 7,
        out_specs=[hbm] * 7,
        scratch_shapes=[pltpu.VMEM(a.shape, a.dtype) for a in args]
        + [
            dma((7,)),
            pltpu.VMEM(sig.shape, BF16),
            pltpu.VMEM(sig.shape, BF16),
            pltpu.VMEM(sig.shape, BF16),
            pltpu.VMEM(w.shape, F32),
            pltpu.VMEM(wb.shape, F32),
            pltpu.VMEM(p.shape, F32),
            pltpu.VMEM(pb.shape, F32),
            dma((7,)),
            field,
            field,
            field,
            field,
            field,
            field,
            field,
            pltpu.VMEM((nc, g, t), F32),
            pltpu.VMEM((nc, g, t), F32),
            pltpu.VMEM((nc, g, t), BF16),
            field32,
            field32,
            field32,
            pltpu.VMEM((2, w.shape[2], g2), BF16),
            pltpu.VMEM((2, g, po), BF16),
            pltpu.VMEM((2, g2, 128), F32),
            pltpu.VMEM((2, po, 128), F32),
            pltpu.VMEM((2, g2, w.shape[2]), F32),
            pltpu.VMEM((2, po, g), F32),
            pltpu.VMEM((2, g2 + po, 128), F32),
            pltpu.VMEM((16, 128), F32),
            pltpu.VMEM((ncor * rows, 128), BF16),
            pltpu.VMEM((ncor - 1, rows, 128), BF16),
            pltpu.VMEM((ntm, rows, 128), BF16),
            pltpu.VMEM((ncor * rows, 128), BF16),
        ]
        + [dma((nc,))] * 8
        + [dma((ncor - 1,))] * 2
        + [dma((ntm - 1,))] * 2
        + [dma((ncor - 1,))] * 2,
        compiler_params=pltpu.CompilerParams(
            collective_id=0, has_side_effects=True, vmem_limit_bytes=room
        ),
        cost_estimate=pl.CostEstimate(
            flops=flops, bytes_accessed=6 * sig.size * 2, transcendentals=2 * g2 * time
        ),
    )(*args)
    return pl.pallas_call(
        deliver,
        out_shape=tuple(jax.ShapeDtypeStruct(a.shape, a.dtype) for a in outs),
        in_specs=[hbm] * 7,
        out_specs=[hbm] * 7,
        scratch_shapes=[pltpu.VMEM(a.shape, a.dtype) for a in outs] + [dma((2, 7))],
        compiler_params=pltpu.CompilerParams(vmem_limit_bytes=room),
    )(*outs)


def solution(mesh):
    field = P("corner", None, "tm")
    return jax.shard_map(
        on_device,
        mesh=mesh,
        in_specs=(field, P(), P(), P(), P(), field, field),
        out_specs=(field, field, field, P(), P(), P(), P()),
        check_vma=False,
    )
```
